32 devices in a mesh: groups: 2 (over x), tensor: 8 (over z, y), dp: 2 (over core).
Axes of the slice: x: 2, y: 2, z: 4, core: 2. Of those that a mesh axis runs over, the one named last changes fastest.
Arguments:
- cotangent: bfloat16 [2048, 8192], P(('groups', 'dp'), 'tensor'), parts along dimension 0, may hold values from -6 to 6
- activations: bfloat16 [2048, 32768], P(('groups', 'dp'), 'tensor'), parts along dimension 0, may hold values from -0.59765625 to 0.59765625
- qweight: int32 [32768, 4096], P('tensor'), may hold values from 0 to 255, as said below
- scales: bfloat16 [512, 8192], P('tensor'), may hold values from 0.0010986328 to 0.0047912598
- adapter_down_weight: bfloat16 [16, 16, 32768], P(('groups', 'tensor')), parts along dimension 0, may hold values from -0.23925781 to 0.23925781
- adapter_up_weight: bfloat16 [16, 16, 8192], P(('groups', 'tensor')), parts along dimension 0, may hold values from -0.0625 to 0.0625
- token_job_index: int32 [2048, 1], P(('groups', 'dp')), parts along dimension 0, may hold values from 0 to 7; in each aligned block of 512 rows (0 to 511, 512 to 1023, ...) at most 256 rows name the same one
- job_slot_owner: int32 [16], P('groups'), parts along dimension 0, may hold values from 0 to 7, each once
Outputs:
- grad_input: bfloat16 [2048, 32768], P(('groups', 'dp'), 'tensor'), parts along dimension 0
- grad_a: float32 [16, 16, 32768], P(('groups', 'tensor'), None, 'dp'), parts along dimension 0
- grad_b: float32 [16, 16, 8192], P(('groups', 'tensor'), None, 'dp'), parts along dimension 0
The draws below stay inside these ranges and needn't reach their ends.
There are 2 independent parts, one for each index of `groups`. The reference program is written for one: setup_inputs(seed, part) draws one part's arguments, and reference() takes and returns one part's arrays. A program takes and returns all parts, laid end to end along the dimension named above; an argument that names none is the same for every part. Nothing has to cross between parts.
Inputs may be any that keep to these rules, and one draw needn't show every extreme that they name: `token_job_index`: among the 512 rows of one index of dp (aligned blocks of rows), no job is named by more than 256 rows; some job is named by exactly 256 rows. `job_slot_owner`: each slot is named once. `qweight`: every word holds two independent codes in its low eight bits.
All inputs are finite; a program needn't handle non-finite values.
Results may differ from the reference program's by a relative error of at most 0.0048.
Values may be sent and summed in bfloat16 or wider, within the bound.
No kernel may reach another device: no remote copies, remote signals or barrier semaphores. Data moves between devices by JAX's collectives and lax.ppermute only.
A program may use at most 960 MiB of HBM per device.

```python
import math
import jax
import jax.numpy as jnp
import numpy as np
from jax import lax

OUTPUT_FEATURES = 8192
HIDDEN_UNITS = 32768
ADAPTER_RANK = 16
GROUP = 64
TOK_DP = 512
ADAPTER_JOBS = 8
CAP = 256
TOKENS = 1024
N_TENSOR = 8


def draw_qweight(key, part):
    key = jax.random.fold_in(key, 11)
    nibbles = jax.random.randint(key, (HIDDEN_UNITS, OUTPUT_FEATURES // 2, 2), 0, 16, dtype=jnp.int32)
    shifts = 4 * jnp.arange(2, dtype=jnp.int32)
    return jnp.sum(jnp.left_shift(nibbles, shifts[None, None, :]), axis=2).astype(jnp.int32)


def levels(rng, shape, cuts, smallest, largest):
    loudness, own = 1.0, jax.random.fold_in(rng, 6)
    for position, blocks in cuts:
        draws = jnp.exp(jax.random.uniform(jax.random.fold_in(own, position), (blocks,), jnp.float32, smallest / len(cuts), largest / len(cuts)))
        loudness = loudness * jnp.repeat(draws, shape[position] // blocks).reshape([-1 if axis == position else 1 for axis in range(len(shape))])
    return loudness


def assign_block(stream_key, own, number, rows, amount, top, reach, slope):
    ranking = jax.random.permutation(stream_key, amount)
    crowded, usual = load_shares(amount, rows * top, reach, slope, True), load_shares(amount, rows * top, reach, slope, False)
    places = jnp.arange(amount)

    def named(sizes, offset_by):
        used = int((sizes > 0).sum())
        fixed = max(1, used // 4)
        passed = fixed + (places - fixed + offset_by * (used - fixed)) % max(1, amount - fixed)
        return jnp.zeros((amount,), jnp.int32).at[ranking[jnp.where(places < fixed, places, passed)]].set(jnp.asarray(sizes, jnp.int32))

    sizes = jnp.where(number % 4 == 0, named(crowded, number // 4), named(usual, number - number // 4 - 1))
    mixed = jax.random.permutation(jax.random.fold_in(own, 3), amount)
    giver, receiver = mixed[0:amount // 2 * 2:2], mixed[1:amount // 2 * 2:2]
    room = jnp.minimum(sizes[giver] - 1, reach - sizes[receiver]) // 2
    room = jnp.where((giver == ranking[0]) | (receiver == ranking[0]) | (sizes[receiver] == 0), 0, jnp.maximum(room, 0))
    passed = jax.random.randint(jax.random.fold_in(own, 4), (amount // 2,), 0, 1 << 20) % (room + 1)
    sizes = sizes.at[giver].add(-passed).at[receiver].add(passed)
    members = jnp.searchsorted(jnp.cumsum(sizes), jnp.arange(rows * top), side="right").astype(jnp.int32)
    grid = members.reshape(top, rows).T
    grid = grid[jax.random.permutation(jax.random.fold_in(own, 1), rows)]
    offset_by = jax.random.randint(jax.random.fold_in(own, 2), (rows, 1), 0, top)
    return jnp.take_along_axis(grid, (jnp.arange(top)[None, :] + offset_by) % top, axis=1)


def load_shares(count, total, bound, skew, full):
    weights = [(1 << 20) // math.isqrt(standing ** skew) + 1 for standing in range(1, count + 1)]
    largest = bound if full else min(bound, max(-(-total // count), total * weights[0] // sum(weights)))
    least = 1 if total - largest >= count - 1 else 0
    counts, surplus = [largest] + [least] * (count - 1), total - largest - least * (count - 1)
    while surplus > 0:
        free = [i for i in range(1, count) if counts[i] < largest] or [i for i in range(1, count) if counts[i] < bound]
        pool, budget = sum([weights[i] for i in free]), surplus
        for i in free:
            extra = min(bound - counts[i], max(1, budget * weights[i] // pool), surplus)
            counts[i] = counts[i] + extra
            surplus = surplus - extra
    return np.array(counts)


def bell_draw(stream_key, extent, scale, bound, pieces=(), held_as=jnp.bfloat16):
    drawn = jax.random.normal(stream_key, extent, jnp.float32) * scale
    if len(pieces) > 0:
        drawn = levels(stream_key, extent, pieces, -0.22, 0.18) * drawn
    return jnp.clip(drawn, min=-bound, max=bound).astype(held_as)


def setup_inputs(seed: int = 0, part: int = 0) -> dict:
    seeds = jax.random.split(jax.random.key(seed), 9)
    part_splits = jax.random.split(jax.random.fold_in(seeds[8], part), 9)
    cotangent = bell_draw(part_splits[0], (TOKENS, OUTPUT_FEATURES), 1.0, 6.0, ((0, 2), (1, 8)))
    activations = bell_draw(part_splits[1], (TOKENS, HIDDEN_UNITS), 0.1, 0.59765625, ((0, 2), (1, 8)))
    qweight = draw_qweight(jax.random.fold_in(seeds[8], 71), part)
    scales = jnp.clip(jnp.exp(math.log(0.0047912598) - 1.47272687 * jax.random.uniform(seeds[3], (HIDDEN_UNITS // GROUP, OUTPUT_FEATURES), jnp.float32) ** levels(seeds[3], (HIDDEN_UNITS // GROUP, OUTPUT_FEATURES), ((0, 8),), -0.2, 0.2)), 0.0010986328, 0.0047912598).astype(jnp.bfloat16)
    adapter_down_weight = bell_draw(part_splits[4], (ADAPTER_JOBS, ADAPTER_RANK, HIDDEN_UNITS), 0.04, 0.23925781, ((0, 8),))
    adapter_up_weight = bell_draw(part_splits[5], (ADAPTER_JOBS, ADAPTER_RANK, OUTPUT_FEATURES), OUTPUT_FEATURES ** -0.5, 0.0625, ((0, 8),))
    token_job_index_keys = jax.random.split(jax.random.fold_in(part_splits[6], 1), TOKENS // TOK_DP)
    token_job_index_turns = jax.random.permutation(jax.random.fold_in(part_splits[6], 3), TOKENS // TOK_DP)
    token_job_index = jax.vmap(lambda own, number: assign_block(jax.random.fold_in(part_splits[6], 2), own, number, TOK_DP, ADAPTER_JOBS, 1, CAP, 2))(token_job_index_keys, token_job_index_turns).reshape((TOKENS, 1))
    job_slot_owner = jax.random.permutation(part_splits[7], ADAPTER_JOBS).astype(jnp.int32)
    return dict(cotangent=cotangent, activations=activations, qweight=qweight, scales=scales, adapter_down_weight=adapter_down_weight, adapter_up_weight=adapter_up_weight, token_job_index=token_job_index, job_slot_owner=job_slot_owner)


def unpack_weight(packed, scale_rows):
    shifts = 4 * jnp.arange(2, dtype=jnp.int32)
    codes = (jnp.right_shift(packed[:, :, None], shifts[None, None, :]) & 15) - 8
    hidden_rows = packed.shape[0]
    width = packed.shape[1] * 2
    codes = codes.reshape(hidden_rows // GROUP, GROUP, width).astype(jnp.float32)
    scaled = codes * scale_rows.astype(jnp.float32)[:, None, :]
    return scaled.reshape(hidden_rows, width).astype(jnp.bfloat16)


def reference(cotangent, activations, qweight, scales, adapter_down_weight, adapter_up_weight, token_job_index, job_slot_owner):
    block_rows = HIDDEN_UNITS // N_TENSOR
    packed_blocks = qweight.reshape(N_TENSOR, block_rows, OUTPUT_FEATURES // 2)
    scale_blocks = scales.reshape(N_TENSOR, block_rows // GROUP, OUTPUT_FEATURES)

    def base_block(pair):
        weight = unpack_weight(pair[0], pair[1])
        return lax.dot_general(cotangent, weight, (((1,), (1,)), ((), ())), preferred_element_type=jnp.float32)

    stacked = lax.map(base_block, (packed_blocks, scale_blocks))
    base_grad = jnp.transpose(stacked, (1, 0, 2)).reshape(TOKENS, HIDDEN_UNITS)
    job_hit = (token_job_index == jnp.arange(ADAPTER_JOBS, dtype=jnp.int32)[None, :]).astype(jnp.int32)
    slot = jnp.sum(job_hit * job_slot_owner[None, :], axis=1)

    def per_slot(carry, slot_index):
        mask = (slot == slot_index)[:, None]
        down_matrix = adapter_down_weight[slot_index]
        up_matrix = adapter_up_weight[slot_index]
        rank_in = lax.dot_general(activations, down_matrix, (((1,), (1,)), ((), ())), preferred_element_type=jnp.float32).astype(jnp.bfloat16)
        rank_out = lax.dot_general(cotangent, up_matrix, (((1,), (1,)), ((), ())), preferred_element_type=jnp.float32).astype(jnp.bfloat16)
        rank_in = jnp.where(mask, rank_in, jnp.zeros_like(rank_in))
        rank_out = jnp.where(mask, rank_out, jnp.zeros_like(rank_out))
        grad_down = 2.0 * jnp.dot(rank_out.T, activations, preferred_element_type=jnp.float32)
        grad_up = 2.0 * jnp.dot(rank_in.T, cotangent, preferred_element_type=jnp.float32)
        low_rank = (2.0 * jnp.dot(rank_out, down_matrix, preferred_element_type=jnp.float32)).astype(jnp.bfloat16)
        return carry + low_rank.astype(jnp.float32), (grad_down, grad_up)

    start_sum = jnp.zeros((TOKENS, HIDDEN_UNITS), jnp.float32)
    low_sum, grads = lax.scan(per_slot, start_sum, jnp.arange(ADAPTER_JOBS, dtype=jnp.int32))
    grad_input = (base_grad + low_sum).astype(jnp.bfloat16)
    return grad_input, grads[0], grads[1]
```

```python
import functools

import jax
import jax.numpy as jnp
from jax import lax
from jax.experimental import pallas as pl
from jax.experimental.pallas import tpu as pltpu
from jax.sharding import PartitionSpec as P

GROUP = 64
CHUNKS = 8
MIB = 2**20
bf16, f32 = jnp.bfloat16, jnp.float32


def params(mib):
    return pltpu.CompilerParams(vmem_limit_bytes=mib * MIB)


def cost(flops, nbytes):
    return pl.CostEstimate(flops=int(flops), bytes_accessed=int(nbytes), transcendentals=0)


def xdot(a, b, ca, cb):
    return lax.dot_general(a, b, (((ca,), (cb,)), ((), ())), preferred_element_type=f32)


def base_kernel(nc, first, last, rows, ids, *refs):
    refs = list(refs)
    c_refs, q_refs, s_refs = refs[:nc], refs[nc : 2 * nc], refs[2 * nc : 3 * nc]
    refs = refs[3 * nc :]
    acc_ref = None if first else refs.pop(0)
    r_ref, d_ref = (refs.pop(0), refs.pop(0)) if last else (None, None)
    out_ref, cd, sd = refs
    width = cd.shape[2]
    step = pl.program_id(0)

    @pl.when(step == 0)
    def _():
        row = lax.broadcasted_iota(jnp.int32, (256, 256), 0)
        col = lax.broadcasted_iota(jnp.int32, (256, 256), 1)
        perm = (row == 2 * (col % 128) + col // 128).astype(f32).astype(bf16)
        for c in range(nc):
            for b in range(width // 256):
                at = slice(b * 256, b * 256 + 256)
                cd[c, :, at] = xdot(c_refs[c][:, at], perm, 1, 0).astype(bf16)
                sd[c, :, at] = xdot(s_refs[c][:, at], perm, 1, 0)

    total = None
    for c in range(nc):
        words = q_refs[c][...]
        srows = sd[c, pl.ds(pl.multiple_of(step * (rows // GROUP), rows // GROUP), rows // GROUP), :]
        parts = []
        for b in range(width // 256):
            word = words[:, b * 128 : b * 128 + 128]
            for half in range(2):
                code = (word & 15) if half == 0 else lax.shift_right_logical(word, 4)
                at = b * 256 + half * 128
                scale = jnp.broadcast_to(
                    srows[:, at : at + 128].astype(bf16)[:, None, :], (rows // GROUP, GROUP, 128)
                ).reshape(rows, 128)
                parts.append((code - 8).astype(bf16) * scale)
        weight = jnp.concatenate(parts, axis=1)
        term = xdot(cd[c], weight, 1, 1)
        total = term if total is None else total + term
    if acc_ref is not None:
        total = total + acc_ref[...]
    if last:
        low = (2.0 * xdot(r_ref[...], d_ref[...], 1, 0)).astype(bf16)
        total = total + low.astype(f32)
    out_ref[...] = total.astype(out_ref.dtype)


def base_step(ids, chunks, q, s, acc=None, adapter=None):
    nc = len(chunks)
    tok, width = chunks[0].shape
    hidden = q.shape[0]
    rows = min(1024, hidden)
    last = adapter is not None
    first = acc is None
    groups = s.shape[0]
    in_specs = [pl.BlockSpec((tok, width), lambda i, ids: (0, 0)) for _ in chunks]
    in_specs += [pl.BlockSpec((rows, width // 2), lambda i, ids, c=c: (i, ids[c])) for c in range(nc)]
    in_specs += [pl.BlockSpec((groups, width), lambda i, ids, c=c: (0, ids[c])) for c in range(nc)]
    args = list(chunks) + [q] * nc + [s] * nc
    aliases = {}
    if not first:
        if not last:
            aliases = {1 + len(args): 0}
        in_specs.append(pl.BlockSpec((tok, rows), lambda i, ids: (0, i)))
        args.append(acc)
    if last:
        ranks = adapter[0].shape[1]
        in_specs.append(pl.BlockSpec((tok, ranks), lambda i, ids: (0, 0)))
        in_specs.append(pl.BlockSpec((ranks, rows), lambda i, ids: (0, i)))
        args += list(adapter)
    nbytes = nc * hidden * width * 2 + (0 if first else tok * hidden * 4) + tok * hidden * 4
    return pl.pallas_call(
        functools.partial(base_kernel, nc, first, last, rows),
        grid_spec=pltpu.PrefetchScalarGridSpec(
            num_scalar_prefetch=1,
            grid=(hidden // rows,),
            in_specs=in_specs,
            out_specs=pl.BlockSpec((tok, rows), lambda i, ids: (0, i)),
            scratch_shapes=[pltpu.VMEM((nc, tok, width), bf16), pltpu.VMEM((nc, groups, width), f32)],
        ),
        out_shape=jax.ShapeDtypeStruct((tok, hidden), bf16 if last else f32),
        input_output_aliases=aliases,
        compiler_params=params(52),
        cost_estimate=cost(2 * nc * tok * hidden * width, nbytes),
    )(ids, *args)


def slots_of(job_ref, owner_ref, jobs):
    tok = job_ref[...]
    slot = jnp.zeros_like(tok)
    for k in range(jobs):
        slot = jnp.where(tok == k, owner_ref[k], slot)
    return slot


def pack_kernel(n, down_ref, up_ref, *outs):
    me = lax.axis_index("tensor")
    dcols, ucols = down_ref.shape[1] // n, up_ref.shape[1] // n
    for r in range(n):
        to = lax.bitwise_xor(me, r)
        outs[r][:, :dcols] = down_ref[:, pl.ds(pl.multiple_of(to * dcols, dcols), dcols)]
        outs[r][:, dcols:] = up_ref[:, pl.ds(pl.multiple_of(to * ucols, ucols), ucols)]


def pack(down, up, n):
    rank = down.shape[0]
    cols = (down.shape[1] + up.shape[1]) // n
    return pl.pallas_call(
        functools.partial(pack_kernel, n),
        out_shape=[jax.ShapeDtypeStruct((rank, cols), bf16)] * n,
        compiler_params=params(24),
        cost_estimate=cost(0, 4 * n * rank * cols),
    )(down, up)


def ranks_kernel(n, rank, owner_ref, job_ref, act_ref, cot_ref, *refs):
    pieces, outs, d_ref = refs[:n], refs[n : 2 * n], refs[2 * n]
    me = lax.axis_index("tensor")
    hidden = act_ref.shape[1]
    slot = slots_of(job_ref, owner_ref, n)
    d_ref[...] = jnp.concatenate([p[:, :hidden] for p in pieces], axis=0)
    up = jnp.concatenate([p[:, hidden:] for p in pieces], axis=0)
    rin = xdot(d_ref[...], act_ref[...], 1, 1)
    rout = xdot(up, cot_ref[...], 1, 1)
    mine = jnp.zeros((rank, rout.shape[1]), f32)
    for r in range(n):
        mine = jnp.where(slot == lax.bitwise_xor(me, r), rout[r * rank : (r + 1) * rank], mine)
    for r in range(n):
        outs[r][:rank] = rin[r * rank : (r + 1) * rank]
        outs[r][rank:] = mine


def ranks(owner, job, act, cot, pieces, rank):
    n = len(pieces)
    tok, hidden = act.shape
    vm = pl.BlockSpec(memory_space=pltpu.VMEM)
    return pl.pallas_call(
        functools.partial(ranks_kernel, n, rank),
        in_specs=[pl.BlockSpec(memory_space=pltpu.SMEM)] + [vm] * (3 + n),
        out_specs=[vm] * (n + 1),
        out_shape=[jax.ShapeDtypeStruct((2 * rank, tok), f32)] * n
        + [jax.ShapeDtypeStruct((n * rank, hidden), bf16)],
        compiler_params=params(40),
        cost_estimate=cost(2 * tok * hidden * n * rank, 2 * tok * hidden + 4 * n * rank * hidden),
    )(owner, job, act, cot, *pieces)


def grads_kernel(n, rank, owner_ref, job_ref, act_ref, *refs):
    parts, (rin_ref, r_ref, keep_ref, send_ref) = refs[:n], refs[n:]
    me, core = lax.axis_index("tensor"), lax.axis_index("dp")
    slot = slots_of(job_ref, owner_ref, n)
    total = parts[0][...]
    for p in parts[1:]:
        total = total + p[...]
    rin_ref[...] = jnp.where(slot == me, total[:rank], 0.0).astype(bf16)
    rout = total[rank:].astype(bf16).astype(f32)
    spread = jnp.concatenate(
        [jnp.where(slot == lax.bitwise_xor(me, r), rout, 0.0) for r in range(n)], axis=0
    )
    r_ref[...] = spread.T.astype(bf16)
    left = spread.astype(bf16)
    half = act_ref.shape[1] // 2
    for ref, which in ((send_ref, 1 - core), (keep_ref, core)):
        cols = pl.ds(pl.multiple_of(which * half, half), half)
        ref[...] = 2.0 * xdot(left, act_ref[:, cols], 1, 0)


def grads(owner, job, act, parts, rank):
    n = len(parts)
    tok, hidden = act.shape
    vm = pl.BlockSpec(memory_space=pltpu.VMEM)
    half = jax.ShapeDtypeStruct((n * rank, hidden // 2), f32)
    return pl.pallas_call(
        functools.partial(grads_kernel, n, rank),
        in_specs=[pl.BlockSpec(memory_space=pltpu.SMEM)] + [vm] * (2 + n),
        out_specs=[vm] * 4,
        out_shape=[
            jax.ShapeDtypeStruct((rank, tok), bf16),
            jax.ShapeDtypeStruct((tok, n * rank), bf16),
            half,
            half,
        ],
        compiler_params=params(40),
        cost_estimate=cost(2 * tok * hidden * n * rank, 2 * tok * hidden + 4 * n * rank * hidden),
    )(owner, job, act, *parts)


def route(n, core, me, r):
    return lax.bitwise_xor(lax.rem(me, n // 2) * 2 + core, r)


def split_kernel(n, rank, keep_ref, got_ref, *outs):
    me, core = lax.axis_index("tensor"), lax.axis_index("dp")
    for r in range(n):
        piece = lax.bitwise_xor(me, route(n, core, me, r))
        at = pl.ds(pl.multiple_of(piece * rank, rank), rank)
        outs[r][...] = (keep_ref[at, :] + got_ref[at, :]).astype(bf16)


def split(keep, got, n, rank):
    return pl.pallas_call(
        functools.partial(split_kernel, n, rank),
        out_shape=[jax.ShapeDtypeStruct((rank, keep.shape[1]), bf16)] * n,
        compiler_params=params(24),
        cost_estimate=cost(keep.size, 10 * keep.size),
    )(keep, got)


def join_kernel(n, *refs):
    parts, out_ref = refs[:n], refs[n]
    me = lax.axis_index("tensor")
    cols = parts[0].shape[1]
    for r in range(n):
        at = lax.bitwise_xor(me, r)
        out_ref[0, :, pl.ds(pl.multiple_of(at * cols, cols), cols)] = parts[r][...].astype(f32)


def join(parts):
    n = len(parts)
    rank, cols = parts[0].shape
    return pl.pallas_call(
        functools.partial(join_kernel, n),
        out_shape=jax.ShapeDtypeStruct((1, rank, n * cols), f32),
        compiler_params=params(24),
        cost_estimate=cost(0, 6 * n * rank * cols),
    )(*parts)


def up_kernel(nc, ids, rin_ref, *refs):
    chunks, out_ref = refs[:nc], refs[-1]
    width = chunks[0].shape[1]
    for c in range(nc):
        at = pl.ds(pl.multiple_of(ids[c] * width, width), width)
        out_ref[:, at] = 2.0 * xdot(rin_ref[...], chunks[c][...], 1, 0)


def up_step(ids, rin, chunks, out=None):
    nc = len(chunks)
    tok, width = chunks[0].shape
    vm = pl.BlockSpec(memory_space=pltpu.VMEM)
    args = [rin] + list(chunks) + ([] if out is None else [out])
    return pl.pallas_call(
        functools.partial(up_kernel, nc),
        in_specs=[pl.BlockSpec(memory_space=pltpu.SMEM)] + [vm] * len(args),
        out_specs=vm,
        out_shape=jax.ShapeDtypeStruct((rin.shape[0], CHUNKS * width), f32),
        input_output_aliases={} if out is None else {len(args): 0},
        compiler_params=params(24),
        cost_estimate=cost(2 * nc * tok * width * 16, nc * tok * width * 2),
    )(ids, *args)


def small_ring(cot, act, q, scales, down, up, job, owner, n):
    rank = down.shape[0]
    ring = list(range(0, n, 2)) + list(range(n - 1, 0, -2))
    forth = [(ring[i], ring[(i + 1) % n]) for i in range(n)]
    back = [(b, a) for a, b in forth]
    table = []
    for j in range(n):
        p = ring.index(j)
        order = [j]
        for h in range(1, n // 2):
            order += [ring[(p - h) % n], ring[(p + h) % n]]
        table.append(order + [ring[(p + n // 2) % n]])
    me = lax.axis_index("tensor")
    ids = lax.dynamic_index_in_dim(jnp.array(table, jnp.int32), me, 0, keepdims=False)
    swap = [(0, 1), (1, 0)]

    def xor(pieces):
        got = [pieces[0]]
        for r in range(1, n):
            got.append(lax.ppermute(pieces[r], "tensor", [(j, j ^ r) for j in range(n)]))
        return got

    job_row = job.reshape(1, -1)
    pieces = xor(pack(down, up, n))
    *parts, down_cols = ranks(owner, job_row, act, cot, pieces, rank)
    rin, spread, keep, send = grads(owner, job_row, act, xor(parts), rank)
    got = lax.ppermute(send, "dp", swap)
    routed = []
    for r, piece in enumerate(split(keep, got, n, rank)):
        pairs = []
        for j in range(n):
            for core in range(2):
                k = ((j % (n // 2)) * 2 + core) ^ r
                pairs.append((j * 2 + core, k * 2 + j // (n // 2)))
        routed.append(lax.ppermute(piece, ("tensor", "dp"), pairs))
    grad_a = join(routed)

    half = cot.shape[0] // 2
    right, left = cot, cot
    acc = base_step(ids[:1], [cot], q, scales)
    seen = [cot]
    for h in range(1, n // 2):
        right = lax.ppermute(right, "tensor", forth)
        left = lax.ppermute(left, "tensor", back)
        acc = base_step(ids[2 * h - 1 : 2 * h + 1], [right, left], q, scales, acc)
        seen += [right, left]
    last = jnp.concatenate(
        [lax.ppermute(right[:half], "tensor", forth), lax.ppermute(left[half:], "tensor", back)], axis=0
    )
    grad_up = up_step(ids, rin, seen)
    grad_up = up_step(ids[n - 1 :], rin, [last], grad_up)
    grad_input = base_step(ids[n - 1 :], [last], q, scales, acc, (spread, down_cols))
    core = lax.axis_index("dp")
    cols = grad_up.shape[1] // 2
    theirs = lax.ppermute(lax.dynamic_slice_in_dim(grad_up, (1 - core) * cols, cols, 1), "dp", swap)
    grad_b = (lax.dynamic_slice_in_dim(grad_up, core * cols, cols, 1) + theirs)[None]
    return grad_input, grad_a, grad_b


def large_ring(cot, act, q, scales, down, up, job, owner, n):
    rank = down.shape[0]
    me = lax.axis_index("tensor")
    jobs = owner.shape[0]
    hit = (job == jnp.arange(jobs, dtype=jnp.int32)[None, :]).astype(jnp.int32)
    slot = jnp.sum(hit * owner[None, :], axis=1)
    full = lax.all_gather(cot, "tensor", axis=1, tiled=True)
    down_cols = lax.all_to_all(
        down.reshape(rank, n, -1), "tensor", split_axis=1, concat_axis=0, tiled=True
    ).reshape(n * rank, -1)
    up_cols = lax.all_to_all(
        up.reshape(rank, n, -1), "tensor", split_axis=1, concat_axis=0, tiled=True
    ).reshape(n * rank, -1)
    mask = jnp.repeat(slot[:, None] == jnp.arange(n, dtype=jnp.int32)[None, :], rank, axis=1)
    rin = lax.psum_scatter(xdot(down_cols, act, 1, 1), "tensor", scatter_dimension=0, tiled=True)
    rin = jnp.where((slot == me)[None, :], rin, 0.0).astype(bf16)
    rout = lax.psum(jnp.where(mask, xdot(cot, up_cols, 1, 1), 0.0), "tensor")
    spread = rout.astype(bf16)
    grad_a = 2.0 * xdot(spread, act, 0, 0)
    grad_a = lax.all_to_all(grad_a, "tensor", split_axis=0, concat_axis=1, tiled=True)
    grad_a = lax.psum_scatter(grad_a, "dp", scatter_dimension=1, tiled=True)[None]
    grad_b = 2.0 * xdot(rin, full, 1, 0)
    grad_b = lax.psum_scatter(grad_b, "dp", scatter_dimension=1, tiled=True)[None]
    width = full.shape[1] // CHUNKS
    ids = jnp.arange(CHUNKS, dtype=jnp.int32)
    chunks = [full[:, c * width : (c + 1) * width] for c in range(CHUNKS)]
    acc = base_step(ids[:2], chunks[:2], q, scales)
    for c in range(2, CHUNKS - 2, 2):
        acc = base_step(ids[c : c + 2], chunks[c : c + 2], q, scales, acc)
    grad_input = base_step(ids[CHUNKS - 2 :], chunks[CHUNKS - 2 :], q, scales, acc, (spread, down_cols))
    return grad_input, grad_a, grad_b


def solution(mesh):
    n = mesh.shape["tensor"]

    def on_device(cot, act, q, scales, down, up, job, owner):
        path = small_ring if n == CHUNKS and mesh.shape["dp"] == 2 else large_ring
        return path(cot, act, q, scales, down[0], up[0], job, owner, n)

    return jax.shard_map(
        on_device,
        mesh=mesh,
        in_specs=(
            P(("groups", "dp"), "tensor"),
            P(("groups", "dp"), "tensor"),
            P("tensor", None),
            P("tensor", None),
            P(("groups", "tensor"), None, None),
            P(("groups", "tensor"), None, None),
            P(("groups", "dp"), None),
            P("groups"),
        ),
        out_specs=(
            P(("groups", "dp"), "tensor"),
            P(("groups", "tensor"), None, "dp"),
            P(("groups", "tensor"), None, "dp"),
        ),
        check_vma=False,
    )
```

```python
import functools

import jax
import jax.numpy as jnp
from jax import lax
from jax.experimental import pallas as pl
from jax.experimental.pallas import tpu as pltpu
from jax.sharding import PartitionSpec as P

GROUP = 64
CHUNKS = 8
MIB = 2**20
bf16, f32 = jnp.bfloat16, jnp.float32
ANY = pl.BlockSpec(memory_space=pl.ANY)
VM = pl.BlockSpec(memory_space=pltpu.VMEM)


def params(mib):
    return pltpu.CompilerParams(vmem_limit_bytes=mib * MIB)


def cost(flops, nbytes):
    return pl.CostEstimate(flops=int(flops), bytes_accessed=int(nbytes), transcendentals=0)


def xdot(a, b, ca, cb):
    return lax.dot_general(a, b, (((ca,), (cb,)), ((), ())), preferred_element_type=f32)


def base_kernel(nc, first, last, low, wide, rows, whole_in, whole_out, ids, *refs):
    refs = list(refs)
    c_refs, q_refs, s_refs = refs[:nc], refs[nc : 2 * nc], refs[2 * nc : 3 * nc]
    refs = refs[3 * nc :]
    acc_ref = None if first else refs.pop(0)
    r_ref, d_ref = (refs.pop(0), refs.pop(0)) if low else (None, None)
    rin_ref = refs.pop(0) if wide else None
    cd, sd = refs[-2:]
    up_ref = refs[-3] if wide else None
    out_ref, token_ref = refs[-5:-3] if wide else refs[-4:-2]
    width = cd.shape[2]
    step = pl.program_id(0)

    @pl.when(step == 0)
    def _():
        row = lax.broadcasted_iota(jnp.int32, (256, 256), 0)
        col = lax.broadcasted_iota(jnp.int32, (256, 256), 1)
        perm = (row == 2 * (col % 128) + col // 128).astype(f32).astype(bf16)
        token_ref[...] = jnp.zeros_like(token_ref)
        for c in range(nc):
            if wide:
                at = pl.ds(pl.multiple_of(ids[c] * width, width), width)
                up_ref[:, at] = 2.0 * xdot(rin_ref[...], c_refs[c][...], 1, 0)
            for b in range(width // 256):
                at = slice(b * 256, b * 256 + 256)
                cd[c, :, at] = xdot(c_refs[c][:, at], perm, 1, 0).astype(bf16)
                sd[c, :, at] = xdot(s_refs[c][:, at], perm, 1, 0)

    total = None
    for c in range(nc):
        words = q_refs[c][...]
        srows = sd[c, pl.ds(pl.multiple_of(step * (rows // GROUP), rows // GROUP), rows // GROUP), :]
        parts = []
        for b in range(width // 256):
            word = words[:, b * 128 : b * 128 + 128]
            for half in range(2):
                code = (word & 15) if half == 0 else lax.shift_right_logical(word, 4)
                at = b * 256 + half * 128
                scale = jnp.broadcast_to(
                    srows[:, at : at + 128].astype(bf16)[:, None, :], (rows // GROUP, GROUP, 128)
                ).reshape(rows, 128)
                parts.append((code - 8).astype(bf16) * scale)
        weight = jnp.concatenate(parts, axis=1)
        term = xdot(cd[c], weight, 1, 1)
        total = term if total is None else total + term
    cols = pl.ds(pl.multiple_of(step * rows, rows), rows)
    if acc_ref is not None:
        total = total + (acc_ref[:, cols] if whole_in else acc_ref[...])
    if low:
        total = total + (2.0 * xdot(r_ref[...], d_ref[...], 1, 0)).astype(bf16).astype(f32)
    if whole_out:
        out_ref[:, cols] = total
    else:
        out_ref[...] = total.astype(out_ref.dtype)


def base_step(ids, chunks, q, s, acc=None, adapter=None, up=None, last=False, after=(), rows=1024, whole=(True, True), limit=24):
    nc = len(chunks)
    tok, width = chunks[0].shape
    hidden = q.shape[0]
    rows = min(rows, hidden)
    first = acc is None
    low, wide = adapter is not None, up is not None
    groups = s.shape[0]
    vm = pl.BlockSpec(memory_space=pltpu.VMEM)
    in_specs = [vm for _ in chunks]
    in_specs += [pl.BlockSpec((rows, width // 2), lambda i, ids, c=c: (i, ids[c])) for c in range(nc)]
    in_specs += [pl.BlockSpec((groups, width), lambda i, ids, c=c: (0, ids[c])) for c in range(nc)]
    args = list(chunks) + [q] * nc + [s] * nc
    aliases = {}
    whole_in, whole_out = whole[0], whole[1] and not last
    block = pl.BlockSpec((tok, rows), lambda i, ids: (0, i))
    if not first:
        if whole_in == whole_out and not last:
            aliases = {1 + len(args): 0}
        in_specs.append(vm if whole_in else block)
        args.append(acc)
    if low:
        ranks = adapter[0].shape[1]
        in_specs.append(pl.BlockSpec((tok, ranks), lambda i, ids: (0, 0)))
        in_specs.append(pl.BlockSpec((ranks, rows), lambda i, ids: (0, i)))
        args += list(adapter)
    out_specs = [
        vm if whole_out else block,
        pl.BlockSpec((8, 128), lambda i, ids: (0, 0)),
    ]
    out_shape = [
        jax.ShapeDtypeStruct((tok, hidden), bf16 if last else f32),
        jax.ShapeDtypeStruct((8, 128), f32),
    ]
    if wide:
        in_specs += [pl.BlockSpec(memory_space=pltpu.VMEM)] * 2
        aliases[2 + len(args)] = 2
        args += list(up)
        out_specs.append(vm)
        out_shape.append(jax.ShapeDtypeStruct(up[1].shape, f32))
    in_specs += [pl.BlockSpec(memory_space=pl.ANY)] * len(after)
    args += list(after)
    return pl.pallas_call(
        functools.partial(base_kernel, nc, first, last, low, wide, rows, whole_in, whole_out),
        grid_spec=pltpu.PrefetchScalarGridSpec(
            num_scalar_prefetch=1,
            grid=(hidden // rows,),
            in_specs=in_specs,
            out_specs=out_specs,
            scratch_shapes=[pltpu.VMEM((nc, tok, width), bf16), pltpu.VMEM((nc, groups, width), f32)],
        ),
        out_shape=out_shape,
        input_output_aliases=aliases,
        compiler_params=params(limit),
        cost_estimate=cost(1000, 1000),
    )(ids, *args)


def slots_of(job_ref, owner_ref, jobs):
    tok = job_ref[...]
    slot = jnp.zeros_like(tok)
    for k in range(jobs):
        slot = jnp.where(tok == k, owner_ref[k], slot)
    return slot


def pack_kernel(n, down_ref, up_ref, out_ref):
    core = lax.axis_index("dp")
    dcols, ucols = down_ref.shape[1] // (2 * n), up_ref.shape[1] // (2 * n)
    for r in range(n):
        at = pl.multiple_of((2 * r + core) * dcols, dcols)
        out_ref[r, :, :dcols] = down_ref[:, pl.ds(at, dcols)]
        at = pl.multiple_of((2 * r + core) * ucols, ucols)
        out_ref[r, :, dcols:] = up_ref[:, pl.ds(at, ucols)]


def pack(down, up, n):
    rank = down.shape[0]
    cols = (down.shape[1] + up.shape[1]) // (2 * n)
    return pl.pallas_call(
        functools.partial(pack_kernel, n),
        out_shape=jax.ShapeDtypeStruct((n, rank, cols), bf16),
        compiler_params=params(16),
        cost_estimate=cost(1000, 1000),
    )(down, up)


def ranks_kernel(n, rank, owner_ref, job_ref, act_ref, cot_ref, own_ref, got_ref, after, *refs):
    keep_ref, send_ref, d_ref, u_ref = refs
    me, core = lax.axis_index("tensor"), lax.axis_index("dp")
    slot = slots_of(job_ref, owner_ref, n)
    dcols, ucols = d_ref.shape[1] // 2, u_ref.shape[1] // 2
    for ref, which in ((own_ref, core), (got_ref, 1 - core)):
        d_ref[:, pl.ds(pl.multiple_of(which * dcols, dcols), dcols)] = ref[:, :, :dcols].reshape(-1, dcols)
        u_ref[:, pl.ds(pl.multiple_of(which * ucols, ucols), ucols)] = ref[:, :, dcols:].reshape(-1, ucols)
    rin = xdot(d_ref[...], act_ref[...], 1, 1)
    rout = xdot(u_ref[...], cot_ref[...], 1, 1)
    mine = jnp.zeros((rank, rout.shape[1]), f32)
    for r in range(n):
        mine = jnp.where(slot == r, rout[r * rank : (r + 1) * rank], mine)
    even = lax.rem(me, 2) == 0
    for z in range(n // 2):
        first = rin[2 * z * rank : (2 * z + 1) * rank]
        second = rin[(2 * z + 1) * rank : (2 * z + 2) * rank]
        keep_ref[z] = jnp.where(even, first, second)
        send_ref[z] = jnp.where(even, second, first)
    keep_ref[n // 2] = mine
    send_ref[n // 2] = mine


def ranks(owner, job, act, cot, own, got, after):
    n, rank, _ = own.shape
    tok, hidden = act.shape
    part = jax.ShapeDtypeStruct((n // 2 + 1, rank, tok), f32)
    return pl.pallas_call(
        functools.partial(ranks_kernel, n, rank),
        in_specs=[pl.BlockSpec(memory_space=pltpu.SMEM)] + [VM] * 5 + [ANY],
        out_specs=[VM] * 3,
        out_shape=[part, part, jax.ShapeDtypeStruct((n * rank, hidden), bf16)],
        scratch_shapes=[pltpu.VMEM((n * rank, cot.shape[1]), bf16)],
        compiler_params=params(16),
        cost_estimate=cost(1000, 1000),
    )(owner, job, act, cot, own, got, after)


def mix_kernel(n, keep_ref, got_ref, after, *outs):
    place = lax.axis_index("tensor") // 2
    rank = keep_ref.shape[1]
    rout = keep_ref[n // 2] + got_ref[n // 2]
    for r in range(n // 2):
        z = lax.bitwise_xor(place, r)
        outs[r][:rank] = keep_ref[z] + got_ref[z]
        outs[r][rank:] = rout


def mix(n, keep, got, after):
    _, rank, tok = keep.shape
    return pl.pallas_call(
        functools.partial(mix_kernel, n),
        in_specs=[VM, VM, ANY],
        out_specs=[VM] * (n // 2),
        out_shape=[jax.ShapeDtypeStruct((2 * rank, tok), f32)] * (n // 2),
        compiler_params=params(16),
        cost_estimate=cost(1000, 1000),
    )(keep, got, after)


def grads_kernel(n, rank, owner_ref, job_ref, act_ref, *refs):
    parts, (rin_ref, r_ref, keep_ref, send_ref) = refs[: n // 2], refs[-4:]
    me, core = lax.axis_index("tensor"), lax.axis_index("dp")
    slot = slots_of(job_ref, owner_ref, n)
    total = parts[0][...]
    for p in parts[1:]:
        total = total + p[...]
    rin_ref[...] = jnp.where(slot == me, total[:rank], 0.0).astype(bf16)
    rout = total[rank:].astype(bf16).astype(f32)
    spread = jnp.concatenate([jnp.where(slot == r, rout, 0.0) for r in range(n)], axis=0)
    r_ref[...] = spread.T.astype(bf16)
    left = spread.astype(bf16)
    half = act_ref.shape[1] // 2
    for ref, which in ((send_ref, 1 - core), (keep_ref, core)):
        cols = pl.ds(pl.multiple_of(which * half, half), half)
        ref[...] = (2.0 * xdot(left, act_ref[:, cols], 1, 0)).reshape(ref.shape)


def grads(owner, job, act, parts, after):
    n, rank = 2 * len(parts), parts[0].shape[0] // 2
    tok, hidden = act.shape
    half = jax.ShapeDtypeStruct((n, rank, hidden // 2), f32)
    return pl.pallas_call(
        functools.partial(grads_kernel, n, rank),
        in_specs=[pl.BlockSpec(memory_space=pltpu.SMEM)] + [VM] * (2 + n // 2) + [ANY],
        out_specs=[VM] * 4,
        out_shape=[
            jax.ShapeDtypeStruct((rank, tok), bf16),
            jax.ShapeDtypeStruct((tok, n * rank), bf16),
            half,
            half,
        ],
        compiler_params=params(16),
        cost_estimate=cost(1000, 1000),
    )(owner, job, act, *parts, after)


def split_kernel(keep_ref, got_ref, after, own_ref, send_ref):
    side = lax.rem(lax.axis_index("tensor"), 2)
    for z in range(own_ref.shape[0]):
        for ref, which in ((own_ref, side), (send_ref, 1 - side)):
            ref[z] = (keep_ref[2 * z + which] + got_ref[2 * z + which]).astype(bf16)


def split(keep, got, after):
    n, rank, cols = keep.shape
    return pl.pallas_call(
        split_kernel,
        in_specs=[VM, VM, ANY],
        out_specs=[VM, VM],
        out_shape=[jax.ShapeDtypeStruct((n // 2, rank, cols), bf16)] * 2,
        compiler_params=params(16),
        cost_estimate=cost(1000, 1000),
    )(keep, got, after)


def merge_kernel(own_ref, got_ref, after, *outs):
    z, core = lax.axis_index("tensor") // 2, lax.axis_index("dp")
    for r, out in enumerate(outs):
        to = lax.bitwise_xor(lax.rem(z, 2) * 2 + core, r)
        out[0] = own_ref[to]
        out[1] = got_ref[to]


def merge(own, got, after):
    rounds, rank, cols = own.shape
    return pl.pallas_call(
        merge_kernel,
        in_specs=[VM, VM, ANY],
        out_specs=[VM] * rounds,
        out_shape=[jax.ShapeDtypeStruct((2, rank, cols), bf16)] * rounds,
        compiler_params=params(16),
        cost_estimate=cost(1000, 1000),
    )(own, got, after)


def join_kernel(*refs):
    parts, out_ref = refs[:-2], refs[-1]
    me = lax.axis_index("tensor")
    cols = parts[0].shape[2]
    for r, part in enumerate(parts):
        source = lax.bitwise_xor(me // 2, r)
        for other in range(2):
            side = lax.bitwise_xor(lax.rem(me, 2), other)
            block = (source // 2) * 2 + side
            at = pl.multiple_of((block * 2 + lax.rem(source, 2)) * cols, cols)
            out_ref[0, :, pl.ds(at, cols)] = part[other].astype(f32)


def join(parts, after):
    _, rank, cols = parts[0].shape
    return pl.pallas_call(
        join_kernel,
        in_specs=[VM] * len(parts) + [ANY],
        out_shape=jax.ShapeDtypeStruct((1, rank, 2 * len(parts) * cols), f32),
        compiler_params=params(16),
        cost_estimate=cost(1000, 1000),
    )(*parts, after)


def tie_kernel(*refs):
    pass


def tie(arrays, after, spec):
    n = len(arrays)
    return pl.pallas_call(
        tie_kernel,
        in_specs=[spec] * n + [ANY],
        out_specs=[spec] * n,
        out_shape=[jax.ShapeDtypeStruct(x.shape, x.dtype) for x in arrays],
        input_output_aliases={i: i for i in range(n)},
        compiler_params=params(16),
        cost_estimate=cost(1000, 1000),
    )(*arrays, after)


def cut_kernel(right_ref, left_ref, after, top_ref, bottom_ref):
    half = top_ref.shape[0]
    top_ref[...] = right_ref[:half]
    bottom_ref[...] = left_ref[half:]


def cut(right, left, after):
    half = jax.ShapeDtypeStruct((right.shape[0] // 2, right.shape[1]), right.dtype)
    return pl.pallas_call(
        cut_kernel,
        in_specs=[VM, VM, ANY],
        out_specs=[VM, VM],
        out_shape=[half, half],
        compiler_params=params(16),
        cost_estimate=cost(1000, 1000),
    )(right, left, after)


def up_kernel(nc, ids, rin_ref, *refs):
    chunks, out_ref = refs[:nc], refs[-1]
    width = chunks[0].shape[1]
    for c in range(nc):
        at = pl.ds(pl.multiple_of(ids[c] * width, width), width)
        out_ref[:, at] = 2.0 * xdot(rin_ref[...], chunks[c][...], 1, 0)


def up_step(ids, rin, chunks, after):
    nc = len(chunks)
    width = chunks[0].shape[1]
    vm = pl.BlockSpec(memory_space=pltpu.VMEM)
    return pl.pallas_call(
        functools.partial(up_kernel, nc),
        in_specs=[pl.BlockSpec(memory_space=pltpu.SMEM)] + [vm] * (nc + 1) + [ANY],
        out_specs=vm,
        out_shape=jax.ShapeDtypeStruct((rin.shape[0], CHUNKS * width), f32),
        compiler_params=params(16),
        cost_estimate=cost(1000, 1000),
    )(ids, rin, *chunks, after)


def up_last_kernel(ids, rin_ref, chunk_ref, up_ref, after, keep_ref, send_ref):
    core = lax.axis_index("dp")
    width = chunk_ref.shape[1]
    half = keep_ref.shape[1]
    each = half // width
    term = 2.0 * xdot(rin_ref[...], chunk_ref[...], 1, 0)
    at = pl.ds(pl.multiple_of(lax.rem(ids[0], each) * width, width), width)
    for ref, which in ((keep_ref, core), (send_ref, 1 - core)):
        ref[...] = up_ref[:, pl.ds(pl.multiple_of(which * half, half), half)]

        @pl.when(ids[0] // each == which)
        def _():
            ref[:, at] = term


def up_last(ids, rin, chunk, up, after):
    vm = pl.BlockSpec(memory_space=pltpu.VMEM)
    half = jax.ShapeDtypeStruct((up.shape[0], up.shape[1] // 2), f32)
    return pl.pallas_call(
        up_last_kernel,
        in_specs=[pl.BlockSpec(memory_space=pltpu.SMEM)] + [vm] * 3 + [ANY],
        out_specs=[vm, vm],
        out_shape=[half, half],
        compiler_params=params(16),
        cost_estimate=cost(1000, 1000),
    )(ids, rin, chunk, up, after)


def small_ring(cot, act, q, scales, down, up, job, owner, n):
    rank = down.shape[0]
    ring = list(range(0, n, 2)) + list(range(n - 1, 0, -2))
    forth = [(ring[i], ring[(i + 1) % n]) for i in range(n)]
    back = [(b, a) for a, b in forth]
    table = []
    for j in range(n):
        p = ring.index(j)
        order = [j]
        for h in range(1, n // 2):
            order += [ring[(p - h) % n], ring[(p + h) % n]]
        table.append(order + [ring[(p + n // 2) % n]])
    me = lax.axis_index("tensor")
    ids = lax.dynamic_index_in_dim(jnp.array(table, jnp.int32), me, 0, keepdims=False)
    swap = [(0, 1), (1, 0)]

    def ring_step(right, left):
        return lax.ppermute(right, "tensor", forth), lax.ppermute(left, "tensor", back)

    def exchange(x):
        return lax.all_to_all(x, "tensor", split_axis=0, concat_axis=0, tiled=True)

    job_row = job.reshape(1, -1)
    def xor(x, r):
        return lax.ppermute(x, "tensor", [(j, j ^ r) for j in range(n)])

    pairs = [ids[2 * h - 1 : 2 * h + 1] for h in range(1, n // 2)]

    right1, left1 = ring_step(cot, cot)
    pieces = exchange(pack(down, up, n))
    other = lax.ppermute(pieces, "dp", swap)
    acc, token = base_step(ids[:1], [cot], q, scales, after=[pieces])
    keep, send, down_cols = ranks(owner, job_row, act, cot, pieces, other, token)
    got = xor(send, 1)

    right1, left1 = tie((right1, left1), down_cols, VM)
    right2, left2 = ring_step(right1, left1)
    acc, token = base_step(pairs[0], [right1, left1], q, scales, acc, after=[down_cols])
    mixed = mix(n, keep, got, token)
    parts = [mixed[0]] + [xor(mixed[r], 2 * r) for r in range(1, n // 2)]

    right2, left2 = tie((right2, left2), mixed[0], VM)
    right3, left3 = ring_step(right2, left2)
    acc, token = base_step(pairs[1], [right2, left2], q, scales, acc, after=[mixed[0]])
    rin, spread, keep, send = grads(owner, job_row, act, parts, token)
    got = lax.ppermute(send, "dp", swap)

    halves = ring_step(*cut(right3, left3, rin))
    grad_up = up_step(ids[:5], rin, [cot, right1, left1, right2, left2], rin)
    own, send = split(keep, got, grad_up)
    got = xor(send, 1)
    acc, token, grad_up = base_step(
        pairs[2], [right3, left3], q, scales, acc, (spread, down_cols), (rin, grad_up), after=[own]
    )
    routed = []
    for r, piece in enumerate(merge(own, got, token)):
        hops = []
        for z in range(n // 2):
            for y in range(2):
                for core in range(2):
                    to = ((z % 2) * 2 + core) ^ r
                    hops.append((z * 4 + y * 2 + core, to * 4 + y * 2 + z // 2))
        routed.append(lax.ppermute(piece, ("tensor", "dp"), hops))
    last = jnp.concatenate(tie(halves, token, VM), axis=0)
    keep, send = up_last(ids[n - 1 :], rin, last, grad_up, token)
    other = lax.ppermute(send, "dp", swap)
    grad_input, token = base_step(ids[n - 1 :], [last], q, scales, acc, last=True, after=[keep])
    grad_a = join(routed, token)
    return grad_input, grad_a, (keep + other)[None]


def large_ring(cot, act, q, scales, down, up, job, owner, n):
    rank = down.shape[0]
    me = lax.axis_index("tensor")
    jobs = owner.shape[0]
    hit = (job == jnp.arange(jobs, dtype=jnp.int32)[None, :]).astype(jnp.int32)
    slot = jnp.sum(hit * owner[None, :], axis=1)
    full = lax.all_gather(cot, "tensor", axis=1, tiled=True)
    down_cols = lax.all_to_all(
        down.reshape(rank, n, -1), "tensor", split_axis=1, concat_axis=0, tiled=True
    ).reshape(n * rank, -1)
    up_cols = lax.all_to_all(
        up.reshape(rank, n, -1), "tensor", split_axis=1, concat_axis=0, tiled=True
    ).reshape(n * rank, -1)
    mask = jnp.repeat(slot[:, None] == jnp.arange(n, dtype=jnp.int32)[None, :], rank, axis=1)
    rin = lax.psum_scatter(xdot(down_cols, act, 1, 1), "tensor", scatter_dimension=0, tiled=True)
    rin = jnp.where((slot == me)[None, :], rin, 0.0).astype(bf16)
    rout = lax.psum(jnp.where(mask, xdot(cot, up_cols, 1, 1), 0.0), "tensor")
    spread = rout.astype(bf16)
    grad_a = 2.0 * xdot(spread, act, 0, 0)
    grad_a = lax.all_to_all(grad_a, "tensor", split_axis=0, concat_axis=1, tiled=True)
    grad_a = lax.psum_scatter(grad_a, "dp", scatter_dimension=1, tiled=True)[None]
    grad_b = 2.0 * xdot(rin, full, 1, 0)
    grad_b = lax.psum_scatter(grad_b, "dp", scatter_dimension=1, tiled=True)[None]
    width = full.shape[1] // CHUNKS
    ids = jnp.arange(CHUNKS, dtype=jnp.int32)
    chunks = [full[:, c * width : (c + 1) * width] for c in range(CHUNKS)]
    acc, _ = base_step(ids[:2], chunks[:2], q, scales)
    for c in range(2, CHUNKS - 2, 2):
        acc, _ = base_step(ids[c : c + 2], chunks[c : c + 2], q, scales, acc)
    grad_input, _ = base_step(
        ids[CHUNKS - 2 :], chunks[CHUNKS - 2 :], q, scales, acc, (spread, down_cols), last=True
    )
    return grad_input, grad_a, grad_b


def solution(mesh):
    n = mesh.shape["tensor"]

    def on_device(cot, act, q, scales, down, up, job, owner):
        path = small_ring if n == CHUNKS == 8 and mesh.shape["dp"] == 2 else large_ring
        return path(cot, act, q, scales, down[0], up[0], job, owner, n)

    return jax.shard_map(
        on_device,
        mesh=mesh,
        in_specs=(
            P(("groups", "dp"), "tensor"),
            P(("groups", "dp"), "tensor"),
            P("tensor", None),
            P("tensor", None),
            P(("groups", "tensor"), None, None),
            P(("groups", "tensor"), None, None),
            P(("groups", "dp"), None),
            P("groups"),
        ),
        out_specs=(
            P(("groups", "dp"), "tensor"),
            P(("groups", "tensor"), None, "dp"),
            P(("groups", "tensor"), None, "dp"),
        ),
        check_vma=False,
    )
```

```python
import functools

import jax
import jax.numpy as jnp
from jax import lax
from jax.experimental import pallas as pl
from jax.experimental.pallas import tpu as pltpu
from jax.sharding import PartitionSpec as P

GROUP = 64
CHUNKS = 8
MIB = 2**20
bf16, f32 = jnp.bfloat16, jnp.float32
ANY = pl.BlockSpec(memory_space=pl.ANY)
VM = pl.BlockSpec(memory_space=pltpu.VMEM)


def params(mib):
    return pltpu.CompilerParams(vmem_limit_bytes=mib * MIB)


def cost(flops, nbytes):
    return pl.CostEstimate(flops=int(flops), bytes_accessed=int(nbytes), transcendentals=0)


def xdot(a, b, ca, cb):
    return lax.dot_general(a, b, (((ca,), (cb,)), ((), ())), preferred_element_type=f32)


def base_kernel(nc, first, last, low, wide, rows, ids, *refs):
    refs = list(refs)
    c_refs, q_refs, s_refs = refs[:nc], refs[nc : 2 * nc], refs[2 * nc : 3 * nc]
    refs = refs[3 * nc :]
    acc_ref = None if first else refs.pop(0)
    r_ref, d_ref = (refs.pop(0), refs.pop(0)) if low else (None, None)
    rin_ref, had_ref = (refs.pop(0), refs.pop(0)) if wide else (None, None)
    cd, sd = refs[-2:]
    up_ref = refs[-3] if wide else None
    out_ref, token_ref = refs[-5:-3] if wide else refs[-4:-2]
    width = cd.shape[1]
    step = pl.program_id(0)

    @pl.when(step == 0)
    def _():
        row = lax.broadcasted_iota(jnp.int32, (256, 256), 0)
        col = lax.broadcasted_iota(jnp.int32, (256, 256), 1)
        perm = (row == 2 * (col % 128) + col // 128).astype(f32).astype(bf16)
        token_ref[...] = jnp.zeros_like(token_ref)
        if wide:
            up_ref[...] = had_ref[...]
        for c in range(nc):
            if wide:
                at = pl.ds(pl.multiple_of(ids[c] * width, width), width)
                up_ref[:, at] = 2.0 * xdot(rin_ref[...], c_refs[c][...], 1, 0)
            for b in range(width // 256):
                at = slice(b * 256, b * 256 + 256)
                cd[c, at] = xdot(perm, c_refs[c][:, at], 0, 1).astype(bf16)
                sd[c, :, at] = xdot(s_refs[c][:, at], perm, 1, 0)

    total = None
    for c in range(nc):
        words = q_refs[c][...]
        srows = sd[c, pl.ds(pl.multiple_of(step * (rows // GROUP), rows // GROUP), rows // GROUP), :]
        parts = []
        for b in range(width // 256):
            word = words[:, b * 128 : b * 128 + 128]
            for half in range(2):
                code = (word & 15) if half == 0 else lax.shift_right_logical(word, 4)
                at = b * 256 + half * 128
                scale = jnp.broadcast_to(
                    srows[:, at : at + 128].astype(bf16)[:, None, :], (rows // GROUP, GROUP, 128)
                ).reshape(rows, 128)
                parts.append((code - 8).astype(bf16) * scale)
        weight = jnp.concatenate(parts, axis=1)
        term = jnp.dot(weight, cd[c], preferred_element_type=f32)
        total = term if total is None else total + term
    at = pl.ds(pl.multiple_of(step * rows, rows), rows)
    if acc_ref is not None:
        total = total + acc_ref[at, :]
    if low:
        total = total + (2.0 * xdot(d_ref[...], r_ref[...], 0, 0)).astype(bf16).astype(f32)
    if last:
        out_ref[...] = total.T.astype(out_ref.dtype)
    else:
        out_ref[at, :] = total


def base_step(ids, chunks, q, s, acc=None, adapter=None, up=None, last=False, after=(), rows=1024):
    nc = len(chunks)
    tok, width = chunks[0].shape
    hidden = q.shape[0]
    rows = min(rows, hidden)
    first = acc is None
    low, wide = adapter is not None, up is not None
    groups = s.shape[0]
    vm = pl.BlockSpec(memory_space=pltpu.VMEM)
    in_specs = [vm for _ in chunks]
    in_specs += [pl.BlockSpec((rows, width // 2), lambda i, ids, c=c: (i, ids[c])) for c in range(nc)]
    in_specs += [pl.BlockSpec((groups, width), lambda i, ids, c=c: (0, ids[c])) for c in range(nc)]
    args = list(chunks) + [q] * nc + [s] * nc
    aliases = {}
    if not first:
        if not last:
            aliases = {1 + len(args): 0}
        in_specs.append(vm)
        args.append(acc)
    if low:
        ranks = adapter[0].shape[0]
        in_specs.append(vm)
        in_specs.append(pl.BlockSpec((ranks, rows), lambda i, ids: (0, i)))
        args += list(adapter)
    out_specs = [
        pl.BlockSpec((tok, rows), lambda i, ids: (0, i)) if last else vm,
        pl.BlockSpec((8, 128), lambda i, ids: (0, 0)),
    ]
    out_shape = [
        jax.ShapeDtypeStruct((tok, hidden), bf16) if last else jax.ShapeDtypeStruct((hidden, tok), f32),
        jax.ShapeDtypeStruct((8, 128), f32),
    ]
    if wide:
        in_specs += [pl.BlockSpec(memory_space=pltpu.VMEM)] * 2
        aliases[2 + len(args)] = 2
        args += list(up)
        out_specs.append(vm)
        out_shape.append(jax.ShapeDtypeStruct(up[1].shape, f32))
    in_specs += [pl.BlockSpec(memory_space=pl.ANY)] * len(after)
    args += list(after)
    return pl.pallas_call(
        functools.partial(base_kernel, nc, first, last, low, wide, rows),
        grid_spec=pltpu.PrefetchScalarGridSpec(
            num_scalar_prefetch=1,
            grid=(hidden // rows,),
            in_specs=in_specs,
            out_specs=out_specs,
            scratch_shapes=[pltpu.VMEM((nc, width, tok), bf16), pltpu.VMEM((nc, groups, width), f32)],
        ),
        out_shape=out_shape,
        input_output_aliases=aliases,
        compiler_params=params(24),
        cost_estimate=cost(2 * nc * tok * hidden * width, 25000000 * nc),
    )(ids, *args)


def slots_of(job_ref, owner_ref, jobs):
    tok = job_ref[...]
    slot = jnp.zeros_like(tok)
    for k in range(jobs):
        slot = jnp.where(tok == k, owner_ref[k], slot)
    return slot


def pack_kernel(n, down_ref, up_ref, out_ref):
    core = lax.axis_index("dp")
    dcols, ucols = down_ref.shape[1] // (2 * n), up_ref.shape[1] // (2 * n)
    for r in range(n):
        at = pl.multiple_of((2 * r + core) * dcols, dcols)
        out_ref[r, :, :dcols] = down_ref[:, pl.ds(at, dcols)]
        at = pl.multiple_of((2 * r + core) * ucols, ucols)
        out_ref[r, :, dcols:] = up_ref[:, pl.ds(at, ucols)]


def pack(down, up, n):
    rank = down.shape[0]
    cols = (down.shape[1] + up.shape[1]) // (2 * n)
    return pl.pallas_call(
        functools.partial(pack_kernel, n),
        out_shape=jax.ShapeDtypeStruct((n, rank, cols), bf16),
        compiler_params=params(16),
        cost_estimate=cost(1000, 4000000),
    )(down, up)


def ranks_kernel(n, rank, owner_ref, job_ref, act_ref, cot_ref, own_ref, got_ref, after, *refs):
    keep_ref, send_ref, d_ref, u_ref = refs
    me, core = lax.axis_index("tensor"), lax.axis_index("dp")
    slot = slots_of(job_ref, owner_ref, n)
    dcols, ucols = d_ref.shape[1] // 2, u_ref.shape[1] // 2
    for ref, which in ((own_ref, core), (got_ref, 1 - core)):
        d_ref[:, pl.ds(pl.multiple_of(which * dcols, dcols), dcols)] = ref[:, :, :dcols].reshape(-1, dcols)
        u_ref[:, pl.ds(pl.multiple_of(which * ucols, ucols), ucols)] = ref[:, :, dcols:].reshape(-1, ucols)
    rin = xdot(d_ref[...], act_ref[...], 1, 1)
    rout = xdot(u_ref[...], cot_ref[...], 1, 1)
    mine = jnp.zeros((rank, rout.shape[1]), f32)
    for r in range(n):
        mine = jnp.where(slot == r, rout[r * rank : (r + 1) * rank], mine)
    even = lax.rem(me, 2) == 0
    for z in range(n // 2):
        first = rin[2 * z * rank : (2 * z + 1) * rank]
        second = rin[(2 * z + 1) * rank : (2 * z + 2) * rank]
        keep_ref[z] = jnp.where(even, first, second)
        send_ref[z] = jnp.where(even, second, first)
    keep_ref[n // 2] = mine
    send_ref[n // 2] = mine


def ranks(owner, job, act, cot, own, got, after):
    n, rank, _ = own.shape
    tok, hidden = act.shape
    part = jax.ShapeDtypeStruct((n // 2 + 1, rank, tok), f32)
    return pl.pallas_call(
        functools.partial(ranks_kernel, n, rank),
        in_specs=[pl.BlockSpec(memory_space=pltpu.SMEM)] + [VM] * 5 + [ANY],
        out_specs=[VM] * 3,
        out_shape=[part, part, jax.ShapeDtypeStruct((n * rank, hidden), bf16)],
        scratch_shapes=[pltpu.VMEM((n * rank, cot.shape[1]), bf16)],
        compiler_params=params(16),
        cost_estimate=cost(1000, 4000000),
    )(owner, job, act, cot, own, got, after)


def mix_kernel(n, keep_ref, got_ref, after, *outs):
    place = lax.axis_index("tensor") // 2
    rank = keep_ref.shape[1]
    rout = keep_ref[n // 2] + got_ref[n // 2]
    for r in range(n // 2):
        z = lax.bitwise_xor(place, r)
        outs[r][:rank] = keep_ref[z] + got_ref[z]
        outs[r][rank:] = rout


def mix(n, keep, got, after):
    _, rank, tok = keep.shape
    return pl.pallas_call(
        functools.partial(mix_kernel, n),
        in_specs=[VM, VM, ANY],
        out_specs=[VM] * (n // 2),
        out_shape=[jax.ShapeDtypeStruct((2 * rank, tok), f32)] * (n // 2),
        compiler_params=params(16),
        cost_estimate=cost(1000, 4000000),
    )(keep, got, after)


def grads_kernel(n, rank, owner_ref, job_ref, act_ref, *refs):
    parts, (rin_ref, r_ref, keep_ref, send_ref) = refs[: n // 2], refs[-4:]
    me, core = lax.axis_index("tensor"), lax.axis_index("dp")
    slot = slots_of(job_ref, owner_ref, n)
    total = parts[0][...]
    for p in parts[1:]:
        total = total + p[...]
    rin_ref[...] = jnp.where(slot == me, total[:rank], 0.0).astype(bf16)
    rout = total[rank:].astype(bf16).astype(f32)
    spread = jnp.concatenate([jnp.where(slot == r, rout, 0.0) for r in range(n)], axis=0)
    left = spread.astype(bf16)
    r_ref[...] = left
    half = act_ref.shape[1] // 2
    for ref, which in ((send_ref, 1 - core), (keep_ref, core)):
        cols = pl.ds(pl.multiple_of(which * half, half), half)
        ref[...] = (2.0 * xdot(left, act_ref[:, cols], 1, 0)).reshape(ref.shape)


def grads(owner, job, act, parts, after):
    n, rank = 2 * len(parts), parts[0].shape[0] // 2
    tok, hidden = act.shape
    half = jax.ShapeDtypeStruct((n, rank, hidden // 2), f32)
    return pl.pallas_call(
        functools.partial(grads_kernel, n, rank),
        in_specs=[pl.BlockSpec(memory_space=pltpu.SMEM)] + [VM] * (2 + n // 2) + [ANY],
        out_specs=[VM] * 4,
        out_shape=[
            jax.ShapeDtypeStruct((rank, tok), bf16),
            jax.ShapeDtypeStruct((n * rank, tok), bf16),
            half,
            half,
        ],
        compiler_params=params(16),
        cost_estimate=cost(1000, 4000000),
    )(owner, job, act, *parts, after)


def split_kernel(keep_ref, got_ref, after, own_ref, send_ref):
    side = lax.rem(lax.axis_index("tensor"), 2)
    for z in range(own_ref.shape[0]):
        for ref, which in ((own_ref, side), (send_ref, 1 - side)):
            ref[z] = (keep_ref[2 * z + which] + got_ref[2 * z + which]).astype(bf16)


def split(keep, got, after):
    n, rank, cols = keep.shape
    return pl.pallas_call(
        split_kernel,
        in_specs=[VM, VM, ANY],
        out_specs=[VM, VM],
        out_shape=[jax.ShapeDtypeStruct((n // 2, rank, cols), bf16)] * 2,
        compiler_params=params(16),
        cost_estimate=cost(1000, 4000000),
    )(keep, got, after)


def merge_kernel(own_ref, got_ref, after, *outs):
    z, core = lax.axis_index("tensor") // 2, lax.axis_index("dp")
    for r, out in enumerate(outs):
        to = lax.bitwise_xor(lax.rem(z, 2) * 2 + core, r)
        out[0] = own_ref[to]
        out[1] = got_ref[to]


def merge(own, got, after):
    rounds, rank, cols = own.shape
    return pl.pallas_call(
        merge_kernel,
        in_specs=[VM, VM, ANY],
        out_specs=[VM] * rounds,
        out_shape=[jax.ShapeDtypeStruct((2, rank, cols), bf16)] * rounds,
        compiler_params=params(16),
        cost_estimate=cost(1000, 4000000),
    )(own, got, after)


def join_kernel(*refs):
    parts, out_ref = refs[:-2], refs[-1]
    me = lax.axis_index("tensor")
    cols = parts[0].shape[2]
    for r, part in enumerate(parts):
        source = lax.bitwise_xor(me // 2, r)
        for other in range(2):
            side = lax.bitwise_xor(lax.rem(me, 2), other)
            block = (source // 2) * 2 + side
            at = pl.multiple_of((block * 2 + lax.rem(source, 2)) * cols, cols)
            out_ref[0, :, pl.ds(at, cols)] = part[other].astype(f32)


def join(parts, after):
    _, rank, cols = parts[0].shape
    return pl.pallas_call(
        join_kernel,
        in_specs=[VM] * len(parts) + [ANY],
        out_shape=jax.ShapeDtypeStruct((1, rank, 2 * len(parts) * cols), f32),
        compiler_params=params(16),
        cost_estimate=cost(1000, 4000000),
    )(*parts, after)


def tie_kernel(*refs):
    pass


def tie(arrays, after):
    n = len(arrays)
    return pl.pallas_call(
        tie_kernel,
        in_specs=[ANY] * (n + 1),
        out_specs=[ANY] * n,
        out_shape=[jax.ShapeDtypeStruct(x.shape, x.dtype) for x in arrays],
        input_output_aliases={i: i for i in range(n)},
        compiler_params=params(16),
        cost_estimate=cost(1000, 1000),
    )(*arrays, after)


def cut_kernel(right_ref, left_ref, after, top_ref, bottom_ref):
    half = top_ref.shape[0]
    top_ref[...] = right_ref[:half]
    bottom_ref[...] = left_ref[half:]


def cut(right, left, after):
    half = jax.ShapeDtypeStruct((right.shape[0] // 2, right.shape[1]), right.dtype)
    return pl.pallas_call(
        cut_kernel,
        in_specs=[VM, VM, ANY],
        out_specs=[VM, VM],
        out_shape=[half, half],
        compiler_params=params(16),
        cost_estimate=cost(1000, 4000000),
    )(right, left, after)


def up_kernel(nc, ids, rin_ref, *refs):
    chunks, out_ref = refs[:nc], refs[-1]
    width = chunks[0].shape[1]
    for c in range(nc):
        at = pl.ds(pl.multiple_of(ids[c] * width, width), width)
        out_ref[:, at] = 2.0 * xdot(rin_ref[...], chunks[c][...], 1, 0)


def up_step(ids, rin, chunks, after):
    nc = len(chunks)
    width = chunks[0].shape[1]
    vm = pl.BlockSpec(memory_space=pltpu.VMEM)
    return pl.pallas_call(
        functools.partial(up_kernel, nc),
        in_specs=[pl.BlockSpec(memory_space=pltpu.SMEM)] + [vm] * (nc + 1) + [ANY],
        out_specs=vm,
        out_shape=jax.ShapeDtypeStruct((rin.shape[0], CHUNKS * width), f32),
        compiler_params=params(16),
        cost_estimate=cost(1000, 4000000),
    )(ids, rin, *chunks, after)


def up_last_kernel(ids, rin_ref, chunk_ref, up_ref, after, keep_ref, send_ref):
    core = lax.axis_index("dp")
    width = chunk_ref.shape[1]
    half = keep_ref.shape[1]
    each = half // width
    term = 2.0 * xdot(rin_ref[...], chunk_ref[...], 1, 0)
    at = pl.ds(pl.multiple_of(lax.rem(ids[0], each) * width, width), width)
    for ref, which in ((keep_ref, core), (send_ref, 1 - core)):
        ref[...] = up_ref[:, pl.ds(pl.multiple_of(which * half, half), half)]

        @pl.when(ids[0] // each == which)
        def _():
            ref[:, at] = term


def up_last(ids, rin, chunk, up, after):
    vm = pl.BlockSpec(memory_space=pltpu.VMEM)
    half = jax.ShapeDtypeStruct((up.shape[0], up.shape[1] // 2), f32)
    return pl.pallas_call(
        up_last_kernel,
        in_specs=[pl.BlockSpec(memory_space=pltpu.SMEM)] + [vm] * 3 + [ANY],
        out_specs=[vm, vm],
        out_shape=[half, half],
        compiler_params=params(16),
        cost_estimate=cost(1000, 4000000),
    )(ids, rin, chunk, up, after)


def small_ring(cot, act, q, scales, down, up, job, owner, n):
    rank = down.shape[0]
    ring = list(range(0, n, 2)) + list(range(n - 1, 0, -2))
    forth = [(ring[i], ring[(i + 1) % n]) for i in range(n)]
    back = [(b, a) for a, b in forth]
    table = []
    for j in range(n):
        p = ring.index(j)
        order = [j]
        for h in range(1, n // 2):
            order += [ring[(p - h) % n], ring[(p + h) % n]]
        table.append(order + [ring[(p + n // 2) % n]])
    me = lax.axis_index("tensor")
    ids = lax.dynamic_index_in_dim(jnp.array(table, jnp.int32), me, 0, keepdims=False)
    swap = [(0, 1), (1, 0)]

    def ring_step(right, left):
        return lax.ppermute(right, "tensor", forth), lax.ppermute(left, "tensor", back)

    def exchange(x):
        return lax.all_to_all(x, "tensor", split_axis=0, concat_axis=0, tiled=True)

    job_row = job.reshape(1, -1)
    def xor(x, r):
        return lax.ppermute(x, "tensor", [(j, j ^ r) for j in range(n)])

    pairs = [ids[2 * h - 1 : 2 * h + 1] for h in range(1, n // 2)]

    right1, left1 = ring_step(cot, cot)
    sent = pack(down, up, n)
    pieces = exchange(sent)
    acc, token = base_step(ids[:1], [cot], q, scales, after=[sent])

    right1, left1 = tie((right1, left1), token)
    right2, left2 = ring_step(right1, left1)
    acc, token = base_step(pairs[0], [right1, left1], q, scales, acc)
    (pieces,) = tie((pieces,), token)
    other = lax.ppermute(pieces, "dp", swap)
    keep, send, down_cols = ranks(owner, job_row, act, cot, pieces, other, token)
    got = xor(send, 1)

    right2, left2 = tie((right2, left2), down_cols)
    right3, left3 = ring_step(right2, left2)
    mixed = mix(n, keep, got, right2)
    parts = [mixed[0]] + [xor(mixed[r], 2 * r) for r in range(1, n // 2)]
    acc, token = base_step(pairs[1], [right2, left2], q, scales, acc, after=[mixed[0]])

    halves = ring_step(*cut(right3, left3, token))
    rin, spread, keep, send = grads(owner, job_row, act, parts, token)
    got = lax.ppermute(send, "dp", swap)
    grad_up = up_step(ids[:5], rin, [cot, right1, left1, right2, left2], rin)
    own, send = split(keep, got, grad_up)
    got = xor(send, 1)
    acc, token, grad_up = base_step(
        pairs[2], [right3, left3], q, scales, acc, (spread, down_cols), (rin, grad_up), after=[own]
    )
    routed = []
    for r, piece in enumerate(merge(own, got, token)):
        hops = []
        for z in range(n // 2):
            for y in range(2):
                for core in range(2):
                    to = ((z % 2) * 2 + core) ^ r
                    hops.append((z * 4 + y * 2 + core, to * 4 + y * 2 + z // 2))
        routed.append(lax.ppermute(piece, ("tensor", "dp"), hops))
    last = jnp.concatenate(tie(halves, token), axis=0)
    keep, send = up_last(ids[n - 1 :], rin, last, grad_up, token)
    other = lax.ppermute(send, "dp", swap)
    grad_input, token = base_step(ids[n - 1 :], [last], q, scales, acc, last=True, after=[keep])
    grad_a = join(routed, token)
    return grad_input, grad_a, (keep + other)[None]


def large_ring(cot, act, q, scales, down, up, job, owner, n):
    rank = down.shape[0]
    me = lax.axis_index("tensor")
    jobs = owner.shape[0]
    hit = (job == jnp.arange(jobs, dtype=jnp.int32)[None, :]).astype(jnp.int32)
    slot = jnp.sum(hit * owner[None, :], axis=1)
    full = lax.all_gather(cot, "tensor", axis=1, tiled=True)
    down_cols = lax.all_to_all(
        down.reshape(rank, n, -1), "tensor", split_axis=1, concat_axis=0, tiled=True
    ).reshape(n * rank, -1)
    up_cols = lax.all_to_all(
        up.reshape(rank, n, -1), "tensor", split_axis=1, concat_axis=0, tiled=True
    ).reshape(n * rank, -1)
    mask = jnp.repeat(slot[:, None] == jnp.arange(n, dtype=jnp.int32)[None, :], rank, axis=1)
    rin = lax.psum_scatter(xdot(down_cols, act, 1, 1), "tensor", scatter_dimension=0, tiled=True)
    rin = jnp.where((slot == me)[None, :], rin, 0.0).astype(bf16)
    rout = lax.psum(jnp.where(mask, xdot(cot, up_cols, 1, 1), 0.0), "tensor")
    spread = rout.astype(bf16)
    grad_a = 2.0 * xdot(spread, act, 0, 0)
    grad_a = lax.all_to_all(grad_a, "tensor", split_axis=0, concat_axis=1, tiled=True)
    grad_a = lax.psum_scatter(grad_a, "dp", scatter_dimension=1, tiled=True)[None]
    grad_b = 2.0 * xdot(rin, full, 1, 0)
    grad_b = lax.psum_scatter(grad_b, "dp", scatter_dimension=1, tiled=True)[None]
    width = full.shape[1] // CHUNKS
    ids = jnp.arange(CHUNKS, dtype=jnp.int32)
    chunks = [full[:, c * width : (c + 1) * width] for c in range(CHUNKS)]
    acc, _ = base_step(ids[:2], chunks[:2], q, scales)
    for c in range(2, CHUNKS - 2, 2):
        acc, _ = base_step(ids[c : c + 2], chunks[c : c + 2], q, scales, acc)
    grad_input, _ = base_step(
        ids[CHUNKS - 2 :], chunks[CHUNKS - 2 :], q, scales, acc, (spread.T, down_cols), last=True
    )
    return grad_input, grad_a, grad_b


def solution(mesh):
    n = mesh.shape["tensor"]

    def on_device(cot, act, q, scales, down, up, job, owner):
        path = small_ring if n == CHUNKS == 8 and mesh.shape["dp"] == 2 else large_ring
        return path(cot, act, q, scales, down[0], up[0], job, owner, n)

    return jax.shard_map(
        on_device,
        mesh=mesh,
        in_specs=(
            P(("groups", "dp"), "tensor"),
            P(("groups", "dp"), "tensor"),
            P("tensor", None),
            P("tensor", None),
            P(("groups", "tensor"), None, None),
            P(("groups", "tensor"), None, None),
            P(("groups", "dp"), None),
            P("groups"),
        ),
        out_specs=(
            P(("groups", "dp"), "tensor"),
            P(("groups", "tensor"), None, "dp"),
            P(("groups", "tensor"), None, "dp"),
        ),
        check_vma=False,
    )
```

```python
import functools

import jax
import jax.numpy as jnp
from jax import lax
from jax.experimental import pallas as pl
from jax.experimental.pallas import tpu as pltpu
from jax.sharding import PartitionSpec as P

GROUP = 64
CHUNKS = 8
MIB = 2**20
bf16, f32 = jnp.bfloat16, jnp.float32
ANY = pl.BlockSpec(memory_space=pl.ANY)
VM = pl.BlockSpec(memory_space=pltpu.VMEM)


def params(mib):
    return pltpu.CompilerParams(vmem_limit_bytes=mib * MIB)


def cost(flops, nbytes):
    return pl.CostEstimate(flops=int(flops), bytes_accessed=int(nbytes), transcendentals=0)


def xdot(a, b, ca, cb):
    return lax.dot_general(a, b, (((ca,), (cb,)), ((), ())), preferred_element_type=f32)


def base_kernel(nc, pieces, first, last, low, wide, rows, ids, *refs):
    refs = list(refs)
    c_refs, refs = refs[:pieces], refs[pieces:]
    q_refs, s_refs = refs[:nc], refs[nc : 2 * nc]
    refs = refs[2 * nc :]
    acc_ref = None if first else refs.pop(0)
    r_ref, d_ref = (refs.pop(0), refs.pop(0)) if low else (None, None)
    rin_ref, had_ref = (refs.pop(0), refs.pop(0)) if wide else (None, None)
    cd, sd = refs[-2:]
    up_ref = refs[-3] if wide else None
    out_ref, token_ref = refs[-5:-3] if wide else refs[-4:-2]
    width = cd.shape[1]
    step = pl.program_id(0)

    @pl.when(step == 0)
    def _():
        row = lax.broadcasted_iota(jnp.int32, (256, 256), 0)
        col = lax.broadcasted_iota(jnp.int32, (256, 256), 1)
        perm = (row == 2 * (col % 128) + col // 128).astype(f32).astype(bf16)
        token_ref[...] = jnp.zeros_like(token_ref)
        if wide:
            up_ref[...] = had_ref[...]
        for c in range(nc):
            if wide:
                at = pl.ds(pl.multiple_of(ids[c] * width, width), width)
                up_ref[:, at] = 2.0 * xdot(rin_ref[...], c_refs[c][...], 1, 0)
            for b in range(width // 256):
                at = slice(b * 256, b * 256 + 256)
                each = pieces // nc
                for p, ref in enumerate(c_refs[c * each : (c + 1) * each]):
                    toks = slice(p * ref.shape[0], (p + 1) * ref.shape[0])
                    cd[c, at, toks] = xdot(perm, ref[:, at], 0, 1).astype(bf16)
                sd[c, :, at] = xdot(s_refs[c][:, at], perm, 1, 0)

    total = None
    for c in range(nc):
        words = q_refs[c][...]
        srows = sd[c, pl.ds(pl.multiple_of(step * (rows // GROUP), rows // GROUP), rows // GROUP), :]
        parts = []
        for b in range(width // 256):
            word = words[:, b * 128 : b * 128 + 128]
            for half in range(2):
                code = (word & 15) if half == 0 else lax.shift_right_logical(word, 4)
                at = b * 256 + half * 128
                scale = jnp.broadcast_to(
                    srows[:, at : at + 128].astype(bf16)[:, None, :], (rows // GROUP, GROUP, 128)
                ).reshape(rows, 128)
                parts.append((code - 8).astype(bf16) * scale)
        weight = jnp.concatenate(parts, axis=1)
        term = jnp.dot(weight, cd[c], preferred_element_type=f32)
        total = term if total is None else total + term
    at = pl.ds(pl.multiple_of(step * rows, rows), rows)
    if acc_ref is not None:
        total = total + acc_ref[at, :]
    if low:
        total = total + (2.0 * xdot(d_ref[...], r_ref[...], 0, 0)).astype(bf16).astype(f32)
    if last:
        out_ref[...] = total.T.astype(out_ref.dtype)
    else:
        out_ref[at, :] = total


def base_step(ids, chunks, q, s, acc=None, adapter=None, up=None, last=False, after=(), rows=1024, nc=None):
    nc = nc or len(chunks)
    tok, width = chunks[0].shape[0] * (len(chunks) // nc), chunks[0].shape[1]
    hidden = q.shape[0]
    rows = min(rows, hidden)
    first = acc is None
    low, wide = adapter is not None, up is not None
    groups = s.shape[0]
    vm = pl.BlockSpec(memory_space=pltpu.VMEM)
    in_specs = [vm for _ in chunks]
    in_specs += [pl.BlockSpec((rows, width // 2), lambda i, ids, c=c: (i, ids[c])) for c in range(nc)]
    in_specs += [pl.BlockSpec((groups, width), lambda i, ids, c=c: (0, ids[c])) for c in range(nc)]
    args = list(chunks) + [q] * nc + [s] * nc
    aliases = {}
    if not first:
        if not last:
            aliases = {1 + len(args): 0}
        in_specs.append(vm)
        args.append(acc)
    if low:
        ranks = adapter[0].shape[0]
        in_specs.append(vm)
        in_specs.append(pl.BlockSpec((ranks, rows), lambda i, ids: (0, i)))
        args += list(adapter)
    out_specs = [
        pl.BlockSpec((tok, rows), lambda i, ids: (0, i)) if last else vm,
        pl.BlockSpec((8, 128), lambda i, ids: (0, 0)),
    ]
    out_shape = [
        jax.ShapeDtypeStruct((tok, hidden), bf16) if last else jax.ShapeDtypeStruct((hidden, tok), f32),
        jax.ShapeDtypeStruct((8, 128), f32),
    ]
    if wide:
        in_specs += [pl.BlockSpec(memory_space=pltpu.VMEM)] * 2
        aliases[2 + len(args)] = 2
        args += list(up)
        out_specs.append(vm)
        out_shape.append(jax.ShapeDtypeStruct(up[1].shape, f32))
    in_specs += [pl.BlockSpec(memory_space=pl.ANY)] * len(after)
    args += list(after)
    return pl.pallas_call(
        functools.partial(base_kernel, nc, len(chunks), first, last, low, wide, rows),
        grid_spec=pltpu.PrefetchScalarGridSpec(
            num_scalar_prefetch=1,
            grid=(hidden // rows,),
            in_specs=in_specs,
            out_specs=out_specs,
            scratch_shapes=[pltpu.VMEM((nc, width, tok), bf16), pltpu.VMEM((nc, groups, width), f32)],
        ),
        out_shape=out_shape,
        input_output_aliases=aliases,
        compiler_params=params(24),
        cost_estimate=cost(2 * nc * tok * hidden * width, 25000000 * nc),
    )(ids, *args)


def slots_of(job_ref, owner_ref, jobs):
    tok = job_ref[...]
    slot = jnp.zeros_like(tok)
    for k in range(jobs):
        slot = jnp.where(tok == k, owner_ref[k], slot)
    return slot


def pack_kernel(n, down_ref, up_ref, out_ref):
    core = lax.axis_index("dp")
    dcols, ucols = down_ref.shape[1] // (2 * n), up_ref.shape[1] // (2 * n)
    for r in range(n):
        at = pl.multiple_of((2 * r + core) * dcols, dcols)
        out_ref[r, :, :dcols] = down_ref[:, pl.ds(at, dcols)]
        at = pl.multiple_of((2 * r + core) * ucols, ucols)
        out_ref[r, :, dcols:] = up_ref[:, pl.ds(at, ucols)]


def pack(down, up, n):
    rank = down.shape[0]
    cols = (down.shape[1] + up.shape[1]) // (2 * n)
    return pl.pallas_call(
        functools.partial(pack_kernel, n),
        out_shape=jax.ShapeDtypeStruct((n, rank, cols), bf16),
        compiler_params=params(16),
        cost_estimate=cost(1000, 4000000),
    )(down, up)


def ranks_kernel(n, rank, owner_ref, job_ref, act_ref, cot_ref, own_ref, got_ref, after, *refs):
    keep_ref, send_ref, d_ref, u_ref = refs
    me, core = lax.axis_index("tensor"), lax.axis_index("dp")
    slot = slots_of(job_ref, owner_ref, n)
    dcols, ucols = d_ref.shape[1] // 2, u_ref.shape[1] // 2
    for ref, which in ((own_ref, core), (got_ref, 1 - core)):
        d_ref[:, pl.ds(pl.multiple_of(which * dcols, dcols), dcols)] = ref[:, :, :dcols].reshape(-1, dcols)
        u_ref[:, pl.ds(pl.multiple_of(which * ucols, ucols), ucols)] = ref[:, :, dcols:].reshape(-1, ucols)
    rin = xdot(d_ref[...], act_ref[...], 1, 1)
    rout = xdot(u_ref[...], cot_ref[...], 1, 1)
    mine = jnp.zeros((rank, rout.shape[1]), f32)
    for r in range(n):
        mine = jnp.where(slot == r, rout[r * rank : (r + 1) * rank], mine)
    even = lax.rem(me, 2) == 0
    for z in range(n // 2):
        first = rin[2 * z * rank : (2 * z + 1) * rank]
        second = rin[(2 * z + 1) * rank : (2 * z + 2) * rank]
        keep_ref[z] = jnp.where(even, first, second)
        send_ref[z] = jnp.where(even, second, first)
    keep_ref[n // 2] = mine
    send_ref[n // 2] = mine


def ranks(owner, job, act, cot, own, got, after):
    n, rank, _ = own.shape
    tok, hidden = act.shape
    part = jax.ShapeDtypeStruct((n // 2 + 1, rank, tok), f32)
    return pl.pallas_call(
        functools.partial(ranks_kernel, n, rank),
        in_specs=[pl.BlockSpec(memory_space=pltpu.SMEM)] + [VM] * 5 + [ANY],
        out_specs=[VM] * 3,
        out_shape=[part, part, jax.ShapeDtypeStruct((n * rank, hidden), bf16)],
        scratch_shapes=[pltpu.VMEM((n * rank, cot.shape[1]), bf16)],
        compiler_params=params(16),
        cost_estimate=cost(1000, 4000000),
    )(owner, job, act, cot, own, got, after)


def mix_kernel(n, keep_ref, got_ref, after, *outs):
    place = lax.axis_index("tensor") // 2
    rank = keep_ref.shape[1]
    rout = keep_ref[n // 2] + got_ref[n // 2]
    for r in range(n // 2):
        z = lax.bitwise_xor(place, r)
        outs[r][:rank] = keep_ref[z] + got_ref[z]
        outs[r][rank:] = rout


def mix(n, keep, got, after):
    _, rank, tok = keep.shape
    return pl.pallas_call(
        functools.partial(mix_kernel, n),
        in_specs=[VM, VM, ANY],
        out_specs=[VM] * (n // 2),
        out_shape=[jax.ShapeDtypeStruct((2 * rank, tok), f32)] * (n // 2),
        compiler_params=params(16),
        cost_estimate=cost(1000, 4000000),
    )(keep, got, after)


def grads_kernel(n, rank, owner_ref, job_ref, act_ref, *refs):
    parts, (rin_ref, r_ref, keep_ref, send_ref) = refs[: n // 2], refs[-4:]
    me, core = lax.axis_index("tensor"), lax.axis_index("dp")
    slot = slots_of(job_ref, owner_ref, n)
    total = parts[0][...]
    for p in parts[1:]:
        total = total + p[...]
    rin_ref[...] = jnp.where(slot == me, total[:rank], 0.0).astype(bf16)
    rout = total[rank:].astype(bf16).astype(f32)
    spread = jnp.concatenate([jnp.where(slot == r, rout, 0.0) for r in range(n)], axis=0)
    left = spread.astype(bf16)
    r_ref[...] = left
    half = act_ref.shape[1] // 2
    for ref, which in ((send_ref, 1 - core), (keep_ref, core)):
        cols = pl.ds(pl.multiple_of(which * half, half), half)
        ref[...] = (2.0 * xdot(left, act_ref[:, cols], 1, 0)).reshape(ref.shape)


def grads(owner, job, act, parts, after):
    n, rank = 2 * len(parts), parts[0].shape[0] // 2
    tok, hidden = act.shape
    half = jax.ShapeDtypeStruct((n, rank, hidden // 2), f32)
    return pl.pallas_call(
        functools.partial(grads_kernel, n, rank),
        in_specs=[pl.BlockSpec(memory_space=pltpu.SMEM)] + [VM] * (2 + n // 2) + [ANY],
        out_specs=[VM] * 4,
        out_shape=[
            jax.ShapeDtypeStruct((rank, tok), bf16),
            jax.ShapeDtypeStruct((n * rank, tok), bf16),
            half,
            half,
        ],
        compiler_params=params(16),
        cost_estimate=cost(1000, 4000000),
    )(owner, job, act, *parts, after)


def split_kernel(keep_ref, got_ref, after, own_ref, send_ref):
    side = lax.rem(lax.axis_index("tensor"), 2)
    for z in range(own_ref.shape[0]):
        for ref, which in ((own_ref, side), (send_ref, 1 - side)):
            ref[z] = (keep_ref[2 * z + which] + got_ref[2 * z + which]).astype(bf16)


def split(keep, got, after):
    n, rank, cols = keep.shape
    return pl.pallas_call(
        split_kernel,
        in_specs=[VM, VM, ANY],
        out_specs=[VM, VM],
        out_shape=[jax.ShapeDtypeStruct((n // 2, rank, cols), bf16)] * 2,
        compiler_params=params(16),
        cost_estimate=cost(1000, 4000000),
    )(keep, got, after)


def merge_kernel(own_ref, got_ref, after, *outs):
    z, core = lax.axis_index("tensor") // 2, lax.axis_index("dp")
    for r, out in enumerate(outs):
        to = lax.bitwise_xor(lax.rem(z, 2) * 2 + core, r)
        out[0] = own_ref[to]
        out[1] = got_ref[to]


def merge(own, got, after):
    rounds, rank, cols = own.shape
    return pl.pallas_call(
        merge_kernel,
        in_specs=[VM, VM, ANY],
        out_specs=[VM] * rounds,
        out_shape=[jax.ShapeDtypeStruct((2, rank, cols), bf16)] * rounds,
        compiler_params=params(16),
        cost_estimate=cost(1000, 4000000),
    )(own, got, after)


def join_kernel(*refs):
    parts, out_ref = refs[:-2], refs[-1]
    me = lax.axis_index("tensor")
    cols = parts[0].shape[2]
    for r, part in enumerate(parts):
        source = lax.bitwise_xor(me // 2, r)
        for other in range(2):
            side = lax.bitwise_xor(lax.rem(me, 2), other)
            block = (source // 2) * 2 + side
            at = pl.multiple_of((block * 2 + lax.rem(source, 2)) * cols, cols)
            out_ref[0, :, pl.ds(at, cols)] = part[other].astype(f32)


def join(parts, after):
    _, rank, cols = parts[0].shape
    return pl.pallas_call(
        join_kernel,
        in_specs=[VM] * len(parts) + [ANY],
        out_shape=jax.ShapeDtypeStruct((1, rank, 2 * len(parts) * cols), f32),
        compiler_params=params(16),
        cost_estimate=cost(1000, 4000000),
    )(*parts, after)


def tie_kernel(*refs):
    pass


def tie(arrays, after):
    n = len(arrays)
    return pl.pallas_call(
        tie_kernel,
        in_specs=[ANY] * (n + 1),
        out_specs=[ANY] * n,
        out_shape=[jax.ShapeDtypeStruct(x.shape, x.dtype) for x in arrays],
        input_output_aliases={i: i for i in range(n)},
        compiler_params=params(16),
        cost_estimate=cost(1000, 1000),
    )(*arrays, after)


def cut_kernel(right_ref, left_ref, after, top_ref, bottom_ref):
    half = top_ref.shape[0]
    top_ref[...] = right_ref[:half]
    bottom_ref[...] = left_ref[half:]


def cut(right, left, after):
    half = jax.ShapeDtypeStruct((right.shape[0] // 2, right.shape[1]), right.dtype)
    return pl.pallas_call(
        cut_kernel,
        in_specs=[VM, VM, ANY],
        out_specs=[VM, VM],
        out_shape=[half, half],
        compiler_params=params(16),
        cost_estimate=cost(1000, 4000000),
    )(right, left, after)


def up_kernel(nc, ids, rin_ref, *refs):
    chunks, out_ref = refs[:nc], refs[-1]
    width = chunks[0].shape[1]
    for c in range(nc):
        at = pl.ds(pl.multiple_of(ids[c] * width, width), width)
        out_ref[:, at] = 2.0 * xdot(rin_ref[...], chunks[c][...], 1, 0)


def up_step(ids, rin, chunks, after):
    nc = len(chunks)
    width = chunks[0].shape[1]
    vm = pl.BlockSpec(memory_space=pltpu.VMEM)
    return pl.pallas_call(
        functools.partial(up_kernel, nc),
        in_specs=[pl.BlockSpec(memory_space=pltpu.SMEM)] + [vm] * (nc + 1) + [ANY],
        out_specs=vm,
        out_shape=jax.ShapeDtypeStruct((rin.shape[0], CHUNKS * width), f32),
        compiler_params=params(16),
        cost_estimate=cost(1000, 4000000),
    )(ids, rin, *chunks, after)


def up_last_kernel(ids, rin_ref, top_ref, bottom_ref, up_ref, after, keep_ref, send_ref):
    core = lax.axis_index("dp")
    toks, width = top_ref.shape
    half = keep_ref.shape[1]
    each = half // width
    term = 2.0 * (xdot(rin_ref[:, :toks], top_ref[...], 1, 0) + xdot(rin_ref[:, toks:], bottom_ref[...], 1, 0))
    at = pl.ds(pl.multiple_of(lax.rem(ids[0], each) * width, width), width)
    for ref, which in ((keep_ref, core), (send_ref, 1 - core)):
        ref[...] = up_ref[:, pl.ds(pl.multiple_of(which * half, half), half)]

        @pl.when(ids[0] // each == which)
        def _():
            ref[:, at] = term


def up_last(ids, rin, halves, up, after):
    vm = pl.BlockSpec(memory_space=pltpu.VMEM)
    half = jax.ShapeDtypeStruct((up.shape[0], up.shape[1] // 2), f32)
    return pl.pallas_call(
        up_last_kernel,
        in_specs=[pl.BlockSpec(memory_space=pltpu.SMEM)] + [vm] * 4 + [ANY],
        out_specs=[vm, vm],
        out_shape=[half, half],
        compiler_params=params(16),
        cost_estimate=cost(1000, 4000000),
    )(ids, rin, *halves, up, after)


def small_ring(cot, act, q, scales, down, up, job, owner, n):
    rank = down.shape[0]
    ring = list(range(0, n, 2)) + list(range(n - 1, 0, -2))
    forth = [(ring[i], ring[(i + 1) % n]) for i in range(n)]
    back = [(b, a) for a, b in forth]
    table = []
    for j in range(n):
        p = ring.index(j)
        order = [j]
        for h in range(1, n // 2):
            order += [ring[(p - h) % n], ring[(p + h) % n]]
        table.append(order + [ring[(p + n // 2) % n]])
    me = lax.axis_index("tensor")
    ids = lax.dynamic_index_in_dim(jnp.array(table, jnp.int32), me, 0, keepdims=False)
    swap = [(0, 1), (1, 0)]

    def ring_step(right, left):
        return lax.ppermute(right, "tensor", forth), lax.ppermute(left, "tensor", back)

    def exchange(x):
        return lax.all_to_all(x, "tensor", split_axis=0, concat_axis=0, tiled=True)

    job_row = job.reshape(1, -1)
    def xor(x, r):
        return lax.ppermute(x, "tensor", [(j, j ^ r) for j in range(n)])

    pairs = [ids[2 * h - 1 : 2 * h + 1] for h in range(1, n // 2)]

    right1, left1 = ring_step(cot, cot)
    sent = pack(down, up, n)
    pieces = exchange(sent)
    acc, token = base_step(ids[:1], [cot], q, scales, after=[sent])

    right1, left1 = tie((right1, left1), token)
    right2, left2 = ring_step(right1, left1)
    acc, token = base_step(pairs[0], [right1, left1], q, scales, acc)
    (pieces,) = tie((pieces,), token)
    other = lax.ppermute(pieces, "dp", swap)
    keep, send, down_cols = ranks(owner, job_row, act, cot, pieces, other, token)
    got = xor(send, 1)

    right2, left2 = tie((right2, left2), down_cols)
    right3, left3 = ring_step(right2, left2)
    mixed = mix(n, keep, got, right2)
    parts = [mixed[0]] + [xor(mixed[r], 2 * r) for r in range(1, n // 2)]
    acc, token = base_step(pairs[1], [right2, left2], q, scales, acc, after=[mixed[0]])

    halves = ring_step(*cut(right3, left3, token))
    rin, spread, keep, send = grads(owner, job_row, act, parts, token)
    got = lax.ppermute(send, "dp", swap)
    grad_up = up_step(ids[:5], rin, [cot, right1, left1, right2, left2], rin)
    own, send = split(keep, got, grad_up)
    got = xor(send, 1)
    acc, token, grad_up = base_step(
        pairs[2], [right3, left3], q, scales, acc, (spread, down_cols), (rin, grad_up), after=[own]
    )
    routed = []
    for r, piece in enumerate(merge(own, got, token)):
        hops = []
        for z in range(n // 2):
            for y in range(2):
                for core in range(2):
                    to = ((z % 2) * 2 + core) ^ r
                    hops.append((z * 4 + y * 2 + core, to * 4 + y * 2 + z // 2))
        routed.append(lax.ppermute(piece, ("tensor", "dp"), hops))
    keep, send = up_last(ids[n - 1 :], rin, halves, grad_up, token)
    other = lax.ppermute(send, "dp", swap)
    grad_input, token = base_step(ids[n - 1 :], halves, q, scales, acc, last=True, after=[keep], nc=1)
    grad_a = join(routed, token)
    return grad_input, grad_a, (keep + other)[None]


def large_ring(cot, act, q, scales, down, up, job, owner, n):
    rank = down.shape[0]
    me = lax.axis_index("tensor")
    jobs = owner.shape[0]
    hit = (job == jnp.arange(jobs, dtype=jnp.int32)[None, :]).astype(jnp.int32)
    slot = jnp.sum(hit * owner[None, :], axis=1)
    full = lax.all_gather(cot, "tensor", axis=1, tiled=True)
    down_cols = lax.all_to_all(
        down.reshape(rank, n, -1), "tensor", split_axis=1, concat_axis=0, tiled=True
    ).reshape(n * rank, -1)
    up_cols = lax.all_to_all(
        up.reshape(rank, n, -1), "tensor", split_axis=1, concat_axis=0, tiled=True
    ).reshape(n * rank, -1)
    mask = jnp.repeat(slot[:, None] == jnp.arange(n, dtype=jnp.int32)[None, :], rank, axis=1)
    rin = lax.psum_scatter(xdot(down_cols, act, 1, 1), "tensor", scatter_dimension=0, tiled=True)
    rin = jnp.where((slot == me)[None, :], rin, 0.0).astype(bf16)
    rout = lax.psum(jnp.where(mask, xdot(cot, up_cols, 1, 1), 0.0), "tensor")
    spread = rout.astype(bf16)
    grad_a = 2.0 * xdot(spread, act, 0, 0)
    grad_a = lax.all_to_all(grad_a, "tensor", split_axis=0, concat_axis=1, tiled=True)
    grad_a = lax.psum_scatter(grad_a, "dp", scatter_dimension=1, tiled=True)[None]
    grad_b = 2.0 * xdot(rin, full, 1, 0)
    grad_b = lax.psum_scatter(grad_b, "dp", scatter_dimension=1, tiled=True)[None]
    width = full.shape[1] // CHUNKS
    ids = jnp.arange(CHUNKS, dtype=jnp.int32)
    chunks = [full[:, c * width : (c + 1) * width] for c in range(CHUNKS)]
    acc, _ = base_step(ids[:2], chunks[:2], q, scales)
    for c in range(2, CHUNKS - 2, 2):
        acc, _ = base_step(ids[c : c + 2], chunks[c : c + 2], q, scales, acc)
    grad_input, _ = base_step(
        ids[CHUNKS - 2 :], chunks[CHUNKS - 2 :], q, scales, acc, (spread.T, down_cols), last=True
    )
    return grad_input, grad_a, grad_b


def solution(mesh):
    n = mesh.shape["tensor"]

    def on_device(cot, act, q, scales, down, up, job, owner):
        path = small_ring if n == CHUNKS == 8 and mesh.shape["dp"] == 2 else large_ring
        return path(cot, act, q, scales, down[0], up[0], job, owner, n)

    return jax.shard_map(
        on_device,
        mesh=mesh,
        in_specs=(
            P(("groups", "dp"), "tensor"),
            P(("groups", "dp"), "tensor"),
            P("tensor", None),
            P("tensor", None),
            P(("groups", "tensor"), None, None),
            P(("groups", "tensor"), None, None),
            P(("groups", "dp"), None),
            P("groups"),
        ),
        out_specs=(
            P(("groups", "dp"), "tensor"),
            P(("groups", "tensor"), None, "dp"),
            P(("groups", "tensor"), None, "dp"),
        ),
        check_vma=False,
    )
```

```python
import functools

import jax
import jax.numpy as jnp
from jax import lax
from jax.experimental import pallas as pl
from jax.experimental.pallas import tpu as pltpu
from jax.sharding import PartitionSpec as P

GROUP = 64
CHUNKS = 8
MIB = 2**20
bf16, f32 = jnp.bfloat16, jnp.float32
ANY = pl.BlockSpec(memory_space=pl.ANY)
VM = pl.BlockSpec(memory_space=pltpu.VMEM)


def params(mib):
    return pltpu.CompilerParams(vmem_limit_bytes=mib * MIB)


def cost(flops, nbytes):
    return pl.CostEstimate(flops=int(flops), bytes_accessed=int(nbytes), transcendentals=0)


def xdot(a, b, ca, cb):
    return lax.dot_general(a, b, (((ca,), (cb,)), ((), ())), preferred_element_type=f32)


def base_kernel(nc, first, last, low, wide, rows, ids, *refs):
    refs = list(refs)
    c_refs, q_refs, s_refs = refs[:nc], refs[nc : 2 * nc], refs[2 * nc : 3 * nc]
    refs = refs[3 * nc :]
    acc_ref = None if first else refs.pop(0)
    r_ref, d_ref = (refs.pop(0), refs.pop(0)) if low else (None, None)
    rin_ref, had_ref = (refs.pop(0), refs.pop(0)) if wide else (None, None)
    cd, sd = refs[-2:]
    up_ref = refs[-3] if wide else None
    out_ref, token_ref = refs[-5:-3] if wide else refs[-4:-2]
    width = cd.shape[1]
    step = pl.program_id(0)

    @pl.when(step == 0)
    def _():
        row = lax.broadcasted_iota(jnp.int32, (256, 256), 0)
        col = lax.broadcasted_iota(jnp.int32, (256, 256), 1)
        perm = (row == 2 * (col % 128) + col // 128).astype(f32).astype(bf16)
        token_ref[...] = jnp.zeros_like(token_ref)
        if wide:
            up_ref[...] = had_ref[...]
        for c in range(nc):
            if wide:
                at = pl.ds(pl.multiple_of(ids[c] * width, width), width)
                up_ref[:, at] = 2.0 * xdot(rin_ref[...], c_refs[c][...], 1, 0)
            for b in range(width // 256):
                at = slice(b * 256, b * 256 + 256)
                cd[c, at] = xdot(perm, c_refs[c][:, at], 0, 1).astype(bf16)
                sd[c, :, at] = xdot(s_refs[c][:, at], perm, 1, 0)

    total = None
    for c in range(nc):
        words = q_refs[c][...]
        srows = sd[c, pl.ds(pl.multiple_of(step * (rows // GROUP), rows // GROUP), rows // GROUP), :]
        parts = []
        for b in range(width // 256):
            word = words[:, b * 128 : b * 128 + 128]
            for half in range(2):
                code = (word & 15) if half == 0 else lax.shift_right_logical(word, 4)
                at = b * 256 + half * 128
                scale = jnp.broadcast_to(
                    srows[:, at : at + 128].astype(bf16)[:, None, :], (rows // GROUP, GROUP, 128)
                ).reshape(rows, 128)
                parts.append((code - 8).astype(bf16) * scale)
        weight = jnp.concatenate(parts, axis=1)
        term = jnp.dot(weight, cd[c], preferred_element_type=f32)
        total = term if total is None else total + term
    at = pl.ds(pl.multiple_of(step * rows, rows), rows)
    if acc_ref is not None:
        total = total + acc_ref[at, :]
    if low:
        total = total + (2.0 * xdot(d_ref[...], r_ref[...], 0, 0)).astype(bf16).astype(f32)
    if last:
        out_ref[...] = total.astype(out_ref.dtype).T
    else:
        out_ref[at, :] = total


def base_step(ids, chunks, q, s, acc=None, adapter=None, up=None, last=False, after=(), rows=1024):
    nc = len(chunks)
    tok, width = chunks[0].shape
    hidden = q.shape[0]
    rows = min(rows, hidden)
    first = acc is None
    low, wide = adapter is not None, up is not None
    groups = s.shape[0]
    vm = pl.BlockSpec(memory_space=pltpu.VMEM)
    in_specs = [vm for _ in chunks]
    in_specs += [pl.BlockSpec((rows, width // 2), lambda i, ids, c=c: (i, ids[c])) for c in range(nc)]
    in_specs += [pl.BlockSpec((groups, width), lambda i, ids, c=c: (0, ids[c])) for c in range(nc)]
    args = list(chunks) + [q] * nc + [s] * nc
    aliases = {}
    if not first:
        if not last:
            aliases = {1 + len(args): 0}
        in_specs.append(vm)
        args.append(acc)
    if low:
        ranks = adapter[0].shape[0]
        in_specs.append(vm)
        in_specs.append(pl.BlockSpec((ranks, rows), lambda i, ids: (0, i)))
        args += list(adapter)
    out_specs = [
        pl.BlockSpec((tok, rows), lambda i, ids: (0, i)) if last else vm,
        pl.BlockSpec((8, 128), lambda i, ids: (0, 0)),
    ]
    out_shape = [
        jax.ShapeDtypeStruct((tok, hidden), bf16) if last else jax.ShapeDtypeStruct((hidden, tok), f32),
        jax.ShapeDtypeStruct((8, 128), f32),
    ]
    if wide:
        in_specs += [pl.BlockSpec(memory_space=pltpu.VMEM)] * 2
        aliases[2 + len(args)] = 2
        args += list(up)
        out_specs.append(vm)
        out_shape.append(jax.ShapeDtypeStruct(up[1].shape, f32))
    in_specs += [pl.BlockSpec(memory_space=pl.ANY)] * len(after)
    args += list(after)
    return pl.pallas_call(
        functools.partial(base_kernel, nc, first, last, low, wide, rows),
        grid_spec=pltpu.PrefetchScalarGridSpec(
            num_scalar_prefetch=1,
            grid=(hidden // rows,),
            in_specs=in_specs,
            out_specs=out_specs,
            scratch_shapes=[pltpu.VMEM((nc, width, tok), bf16), pltpu.VMEM((nc, groups, width), f32)],
        ),
        out_shape=out_shape,
        input_output_aliases=aliases,
        compiler_params=params(24),
        cost_estimate=cost(2 * nc * tok * hidden * width, 25000000 * nc),
    )(ids, *args)


def slots_of(job_ref, owner_ref, jobs):
    tok = job_ref[...]
    slot = jnp.zeros_like(tok)
    for k in range(jobs):
        slot = jnp.where(tok == k, owner_ref[k], slot)
    return slot


def pack_kernel(n, down_ref, up_ref, out_ref):
    core = lax.axis_index("dp")
    dcols, ucols = down_ref.shape[1] // (2 * n), up_ref.shape[1] // (2 * n)
    for r in range(n):
        at = pl.multiple_of((2 * r + core) * dcols, dcols)
        out_ref[r, :, :dcols] = down_ref[:, pl.ds(at, dcols)]
        at = pl.multiple_of((2 * r + core) * ucols, ucols)
        out_ref[r, :, dcols:] = up_ref[:, pl.ds(at, ucols)]


def pack(down, up, n):
    rank = down.shape[0]
    cols = (down.shape[1] + up.shape[1]) // (2 * n)
    return pl.pallas_call(
        functools.partial(pack_kernel, n),
        out_shape=jax.ShapeDtypeStruct((n, rank, cols), bf16),
        compiler_params=params(16),
        cost_estimate=cost(1000, 4000000),
    )(down, up)


def ranks_kernel(n, rank, owner_ref, job_ref, act_ref, cot_ref, own_ref, got_ref, after, *refs):
    keep_ref, send_ref, d_ref, u_ref = refs
    me, core = lax.axis_index("tensor"), lax.axis_index("dp")
    slot = slots_of(job_ref, owner_ref, n)
    dcols, ucols = d_ref.shape[1] // 2, u_ref.shape[1] // 2
    for ref, which in ((own_ref, core), (got_ref, 1 - core)):
        d_ref[:, pl.ds(pl.multiple_of(which * dcols, dcols), dcols)] = ref[:, :, :dcols].reshape(-1, dcols)
        u_ref[:, pl.ds(pl.multiple_of(which * ucols, ucols), ucols)] = ref[:, :, dcols:].reshape(-1, ucols)
    rin = xdot(d_ref[...], act_ref[...], 1, 1)
    rout = xdot(u_ref[...], cot_ref[...], 1, 1)
    mine = jnp.zeros((rank, rout.shape[1]), f32)
    for r in range(n):
        mine = jnp.where(slot == r, rout[r * rank : (r + 1) * rank], mine)
    even = lax.rem(me, 2) == 0
    for z in range(n // 2):
        first = rin[2 * z * rank : (2 * z + 1) * rank]
        second = rin[(2 * z + 1) * rank : (2 * z + 2) * rank]
        keep_ref[z] = jnp.where(even, first, second)
        send_ref[z] = jnp.where(even, second, first)
    keep_ref[n // 2] = mine
    send_ref[n // 2] = mine


def ranks(owner, job, act, cot, own, got, after):
    n, rank, _ = own.shape
    tok, hidden = act.shape
    part = jax.ShapeDtypeStruct((n // 2 + 1, rank, tok), f32)
    return pl.pallas_call(
        functools.partial(ranks_kernel, n, rank),
        in_specs=[pl.BlockSpec(memory_space=pltpu.SMEM)] + [VM] * 5 + [ANY],
        out_specs=[VM] * 3,
        out_shape=[part, part, jax.ShapeDtypeStruct((n * rank, hidden), bf16)],
        scratch_shapes=[pltpu.VMEM((n * rank, cot.shape[1]), bf16)],
        compiler_params=params(16),
        cost_estimate=cost(1000, 4000000),
    )(owner, job, act, cot, own, got, after)


def mix_kernel(n, keep_ref, got_ref, after, *outs):
    place = lax.axis_index("tensor") // 2
    rank = keep_ref.shape[1]
    rout = keep_ref[n // 2] + got_ref[n // 2]
    for r in range(n // 2):
        z = lax.bitwise_xor(place, r)
        outs[r][:rank] = keep_ref[z] + got_ref[z]
        outs[r][rank:] = rout


def mix(n, keep, got, after):
    _, rank, tok = keep.shape
    return pl.pallas_call(
        functools.partial(mix_kernel, n),
        in_specs=[VM, VM, ANY],
        out_specs=[VM] * (n // 2),
        out_shape=[jax.ShapeDtypeStruct((2 * rank, tok), f32)] * (n // 2),
        compiler_params=params(16),
        cost_estimate=cost(1000, 4000000),
    )(keep, got, after)


def grads_kernel(n, rank, owner_ref, job_ref, act_ref, *refs):
    parts, (rin_ref, r_ref, keep_ref, send_ref) = refs[: n // 2], refs[-4:]
    me, core = lax.axis_index("tensor"), lax.axis_index("dp")
    slot = slots_of(job_ref, owner_ref, n)
    total = parts[0][...]
    for p in parts[1:]:
        total = total + p[...]
    rin_ref[...] = jnp.where(slot == me, total[:rank], 0.0).astype(bf16)
    rout = total[rank:].astype(bf16).astype(f32)
    spread = jnp.concatenate([jnp.where(slot == r, rout, 0.0) for r in range(n)], axis=0)
    left = spread.astype(bf16)
    r_ref[...] = left
    half = act_ref.shape[1] // 2
    for ref, which in ((send_ref, 1 - core), (keep_ref, core)):
        cols = pl.ds(pl.multiple_of(which * half, half), half)
        ref[...] = (2.0 * xdot(left, act_ref[:, cols], 1, 0)).reshape(ref.shape)


def grads(owner, job, act, parts, after):
    n, rank = 2 * len(parts), parts[0].shape[0] // 2
    tok, hidden = act.shape
    half = jax.ShapeDtypeStruct((n, rank, hidden // 2), f32)
    return pl.pallas_call(
        functools.partial(grads_kernel, n, rank),
        in_specs=[pl.BlockSpec(memory_space=pltpu.SMEM)] + [VM] * (2 + n // 2) + [ANY],
        out_specs=[VM] * 4,
        out_shape=[
            jax.ShapeDtypeStruct((rank, tok), bf16),
            jax.ShapeDtypeStruct((n * rank, tok), bf16),
            half,
            half,
        ],
        compiler_params=params(16),
        cost_estimate=cost(1000, 4000000),
    )(owner, job, act, *parts, after)


def split_kernel(keep_ref, got_ref, after, own_ref, send_ref):
    side = lax.rem(lax.axis_index("tensor"), 2)
    for z in range(own_ref.shape[0]):
        for ref, which in ((own_ref, side), (send_ref, 1 - side)):
            ref[z] = (keep_ref[2 * z + which] + got_ref[2 * z + which]).astype(bf16)


def split(keep, got, after):
    n, rank, cols = keep.shape
    return pl.pallas_call(
        split_kernel,
        in_specs=[VM, VM, ANY],
        out_specs=[VM, VM],
        out_shape=[jax.ShapeDtypeStruct((n // 2, rank, cols), bf16)] * 2,
        compiler_params=params(16),
        cost_estimate=cost(1000, 4000000),
    )(keep, got, after)


def merge_kernel(own_ref, got_ref, after, *outs):
    z, core = lax.axis_index("tensor") // 2, lax.axis_index("dp")
    for r, out in enumerate(outs):
        to = lax.bitwise_xor(lax.rem(z, 2) * 2 + core, r)
        out[0] = own_ref[to]
        out[1] = got_ref[to]


def merge(own, got, after):
    rounds, rank, cols = own.shape
    return pl.pallas_call(
        merge_kernel,
        in_specs=[VM, VM, ANY],
        out_specs=[VM] * rounds,
        out_shape=[jax.ShapeDtypeStruct((2, rank, cols), bf16)] * rounds,
        compiler_params=params(16),
        cost_estimate=cost(1000, 4000000),
    )(own, got, after)


def join_kernel(*refs):
    parts, out_ref = refs[:-2], refs[-1]
    me = lax.axis_index("tensor")
    cols = parts[0].shape[2]
    for r, part in enumerate(parts):
        source = lax.bitwise_xor(me // 2, r)
        for other in range(2):
            side = lax.bitwise_xor(lax.rem(me, 2), other)
            block = (source // 2) * 2 + side
            at = pl.multiple_of((block * 2 + lax.rem(source, 2)) * cols, cols)
            out_ref[0, :, pl.ds(at, cols)] = part[other].astype(f32)


def join(parts, after):
    _, rank, cols = parts[0].shape
    return pl.pallas_call(
        join_kernel,
        in_specs=[VM] * len(parts) + [ANY],
        out_shape=jax.ShapeDtypeStruct((1, rank, 2 * len(parts) * cols), f32),
        compiler_params=params(16),
        cost_estimate=cost(1000, 4000000),
    )(*parts, after)


def tie_kernel(*refs):
    pass


def tie(arrays, after):
    n = len(arrays)
    return pl.pallas_call(
        tie_kernel,
        in_specs=[ANY] * (n + 1),
        out_specs=[ANY] * n,
        out_shape=[jax.ShapeDtypeStruct(x.shape, x.dtype) for x in arrays],
        input_output_aliases={i: i for i in range(n)},
        compiler_params=params(16),
        cost_estimate=cost(1000, 1000),
    )(*arrays, after)


def cut_kernel(right_ref, left_ref, after, top_ref, bottom_ref):
    half = top_ref.shape[0]
    top_ref[...] = right_ref[:half]
    bottom_ref[...] = left_ref[half:]


def cut(right, left, after):
    half = jax.ShapeDtypeStruct((right.shape[0] // 2, right.shape[1]), right.dtype)
    return pl.pallas_call(
        cut_kernel,
        in_specs=[VM, VM, ANY],
        out_specs=[VM, VM],
        out_shape=[half, half],
        compiler_params=params(16),
        cost_estimate=cost(1000, 4000000),
    )(right, left, after)


def up_kernel(nc, ids, rin_ref, *refs):
    chunks, out_ref = refs[:nc], refs[-1]
    width = chunks[0].shape[1]
    for c in range(nc):
        at = pl.ds(pl.multiple_of(ids[c] * width, width), width)
        out_ref[:, at] = 2.0 * xdot(rin_ref[...], chunks[c][...], 1, 0)


def up_step(ids, rin, chunks, after):
    nc = len(chunks)
    width = chunks[0].shape[1]
    vm = pl.BlockSpec(memory_space=pltpu.VMEM)
    return pl.pallas_call(
        functools.partial(up_kernel, nc),
        in_specs=[pl.BlockSpec(memory_space=pltpu.SMEM)] + [vm] * (nc + 1) + [ANY],
        out_specs=vm,
        out_shape=jax.ShapeDtypeStruct((rin.shape[0], CHUNKS * width), f32),
        compiler_params=params(16),
        cost_estimate=cost(1000, 4000000),
    )(ids, rin, *chunks, after)


def up_last_kernel(ids, rin_ref, chunk_ref, up_ref, after, keep_ref, send_ref):
    core = lax.axis_index("dp")
    width = chunk_ref.shape[1]
    half = keep_ref.shape[1]
    each = half // width
    term = 2.0 * xdot(rin_ref[...], chunk_ref[...], 1, 0)
    at = pl.ds(pl.multiple_of(lax.rem(ids[0], each) * width, width), width)
    for ref, which in ((keep_ref, core), (send_ref, 1 - core)):
        ref[...] = up_ref[:, pl.ds(pl.multiple_of(which * half, half), half)]

        @pl.when(ids[0] // each == which)
        def _():
            ref[:, at] = term


def up_last(ids, rin, chunk, up, after):
    vm = pl.BlockSpec(memory_space=pltpu.VMEM)
    half = jax.ShapeDtypeStruct((up.shape[0], up.shape[1] // 2), f32)
    return pl.pallas_call(
        up_last_kernel,
        in_specs=[pl.BlockSpec(memory_space=pltpu.SMEM)] + [vm] * 3 + [ANY],
        out_specs=[vm, vm],
        out_shape=[half, half],
        compiler_params=params(16),
        cost_estimate=cost(1000, 4000000),
    )(ids, rin, chunk, up, after)


def small_ring(cot, act, q, scales, down, up, job, owner, n):
    rank = down.shape[0]
    ring = list(range(0, n, 2)) + list(range(n - 1, 0, -2))
    forth = [(ring[i], ring[(i + 1) % n]) for i in range(n)]
    back = [(b, a) for a, b in forth]
    table = []
    for j in range(n):
        p = ring.index(j)
        order = [j]
        for h in range(1, n // 2):
            order += [ring[(p - h) % n], ring[(p + h) % n]]
        table.append(order + [ring[(p + n // 2) % n]])
    me = lax.axis_index("tensor")
    ids = lax.dynamic_index_in_dim(jnp.array(table, jnp.int32), me, 0, keepdims=False)
    swap = [(0, 1), (1, 0)]

    def ring_step(right, left):
        return lax.ppermute(right, "tensor", forth), lax.ppermute(left, "tensor", back)

    def exchange(x):
        return lax.all_to_all(x, "tensor", split_axis=0, concat_axis=0, tiled=True)

    job_row = job.reshape(1, -1)
    def xor(x, r):
        return lax.ppermute(x, "tensor", [(j, j ^ r) for j in range(n)])

    pairs = [ids[2 * h - 1 : 2 * h + 1] for h in range(1, n // 2)]

    right1, left1 = ring_step(cot, cot)
    sent = pack(down, up, n)
    pieces = exchange(sent)
    acc, token = base_step(ids[:1], [cot], q, scales, after=[sent])

    right1, left1 = tie((right1, left1), token)
    right2, left2 = ring_step(right1, left1)
    acc, token = base_step(pairs[0], [right1, left1], q, scales, acc)
    (pieces,) = tie((pieces,), token)
    other = lax.ppermute(pieces, "dp", swap)
    keep, send, down_cols = ranks(owner, job_row, act, cot, pieces, other, token)
    got = xor(send, 1)

    right2, left2 = tie((right2, left2), down_cols)
    right3, left3 = ring_step(right2, left2)
    mixed = mix(n, keep, got, right2)
    parts = [mixed[0]] + [xor(mixed[r], 2 * r) for r in range(1, n // 2)]
    acc, token = base_step(pairs[1], [right2, left2], q, scales, acc, after=[mixed[0]])

    halves = ring_step(*cut(right3, left3, token))
    rin, spread, keep, send = grads(owner, job_row, act, parts, token)
    got = lax.ppermute(send, "dp", swap)
    grad_up = up_step(ids[:5], rin, [cot, right1, left1, right2, left2], rin)
    own, send = split(keep, got, grad_up)
    got = xor(send, 1)
    acc, token, grad_up = base_step(
        pairs[2], [right3, left3], q, scales, acc, (spread, down_cols), (rin, grad_up), after=[own]
    )
    routed = []
    for r, piece in enumerate(merge(own, got, token)):
        hops = []
        for z in range(n // 2):
            for y in range(2):
                for core in range(2):
                    to = ((z % 2) * 2 + core) ^ r
                    hops.append((z * 4 + y * 2 + core, to * 4 + y * 2 + z // 2))
        routed.append(lax.ppermute(piece, ("tensor", "dp"), hops))
    last = jnp.concatenate(tie(halves, token), axis=0)
    keep, send = up_last(ids[n - 1 :], rin, last, grad_up, token)
    other = lax.ppermute(send, "dp", swap)
    grad_input, token = base_step(ids[n - 1 :], [last], q, scales, acc, last=True, after=[keep])
    grad_a = join(routed, token)
    return grad_input, grad_a, (keep + other)[None]


def large_ring(cot, act, q, scales, down, up, job, owner, n):
    rank = down.shape[0]
    me = lax.axis_index("tensor")
    jobs = owner.shape[0]
    hit = (job == jnp.arange(jobs, dtype=jnp.int32)[None, :]).astype(jnp.int32)
    slot = jnp.sum(hit * owner[None, :], axis=1)
    full = lax.all_gather(cot, "tensor", axis=1, tiled=True)
    down_cols = lax.all_to_all(
        down.reshape(rank, n, -1), "tensor", split_axis=1, concat_axis=0, tiled=True
    ).reshape(n * rank, -1)
    up_cols = lax.all_to_all(
        up.reshape(rank, n, -1), "tensor", split_axis=1, concat_axis=0, tiled=True
    ).reshape(n * rank, -1)
    mask = jnp.repeat(slot[:, None] == jnp.arange(n, dtype=jnp.int32)[None, :], rank, axis=1)
    rin = lax.psum_scatter(xdot(down_cols, act, 1, 1), "tensor", scatter_dimension=0, tiled=True)
    rin = jnp.where((slot == me)[None, :], rin, 0.0).astype(bf16)
    rout = lax.psum(jnp.where(mask, xdot(cot, up_cols, 1, 1), 0.0), "tensor")
    spread = rout.astype(bf16)
    grad_a = 2.0 * xdot(spread, act, 0, 0)
    grad_a = lax.all_to_all(grad_a, "tensor", split_axis=0, concat_axis=1, tiled=True)
    grad_a = lax.psum_scatter(grad_a, "dp", scatter_dimension=1, tiled=True)[None]
    grad_b = 2.0 * xdot(rin, full, 1, 0)
    grad_b = lax.psum_scatter(grad_b, "dp", scatter_dimension=1, tiled=True)[None]
    width = full.shape[1] // CHUNKS
    ids = jnp.arange(CHUNKS, dtype=jnp.int32)
    chunks = [full[:, c * width : (c + 1) * width] for c in range(CHUNKS)]
    acc, _ = base_step(ids[:2], chunks[:2], q, scales)
    for c in range(2, CHUNKS - 2, 2):
        acc, _ = base_step(ids[c : c + 2], chunks[c : c + 2], q, scales, acc)
    grad_input, _ = base_step(
        ids[CHUNKS - 2 :], chunks[CHUNKS - 2 :], q, scales, acc, (spread.T, down_cols), last=True
    )
    return grad_input, grad_a, grad_b


def solution(mesh):
    n = mesh.shape["tensor"]

    def on_device(cot, act, q, scales, down, up, job, owner):
        path = small_ring if n == CHUNKS == 8 and mesh.shape["dp"] == 2 else large_ring
        return path(cot, act, q, scales, down[0], up[0], job, owner, n)

    return jax.shard_map(
        on_device,
        mesh=mesh,
        in_specs=(
            P(("groups", "dp"), "tensor"),
            P(("groups", "dp"), "tensor"),
            P("tensor", None),
            P("tensor", None),
            P(("groups", "tensor"), None, None),
            P(("groups", "tensor"), None, None),
            P(("groups", "dp"), None),
            P("groups"),
        ),
        out_specs=(
            P(("groups", "dp"), "tensor"),
            P(("groups", "tensor"), None, "dp"),
            P(("groups", "tensor"), None, "dp"),
        ),
        check_vma=False,
    )
```
